256 devices in a mesh: seq: 32 (over x, z), head: 8 (over y, core).
Axes of the slice: x: 4, y: 4, z: 8, core: 2. Of those that a mesh axis runs over, the one named last changes fastest.
Arguments:
- q_codes: bfloat16 [16384, 4096], P(('seq', 'head')), may hold values from -32 to 32
- q_exps: int32 [16384, 32], P(('seq', 'head')), may hold values from -1 to 1
- k_codes: bfloat16 [16384, 4096], P(('seq', 'head')), may hold values from -32 to 32
- k_exps: int32 [16384, 32], P(('seq', 'head')), may hold values from -1 to 1
- v_codes: bfloat16 [16384, 4096], P(('seq', 'head')), may hold values from -6 to 6
- v_exps: int32 [16384, 32], P(('seq', 'head')), may hold values from -1 to 1
- lin_query: bfloat16 [16384, 4096], P('seq', 'head'), may hold values from -6 to 6
- lin_keys: bfloat16 [16384, 4096], P('seq', 'head'), may hold values from -6 to 6
- lin_values: bfloat16 [16384, 4096], P('seq', 'head'), may hold values from -6 to 6
- decay_log: float32 [16384, 32], P('seq', 'head'), may hold values from -1 to 0
Outputs:
- soft_out: bfloat16 [16384, 4096], P(('seq', 'head'))
- lin_out: bfloat16 [16384, 4096], P('seq', 'head')
The draws below stay inside these ranges and needn't reach their ends.
All inputs are finite; a program needn't handle non-finite values.
Results may differ from the reference program's by a relative error of at most 0.02.
Values may be sent and summed in bfloat16 or wider, within the bound.
No kernel may reach another device: no remote copies, remote signals or barrier semaphores. Data moves between devices by JAX's collectives and lax.ppermute only.
A program may use at most 192 MiB of HBM per device.

```python
import math
import jax
import jax.numpy as jnp
from jax import lax

HS = 32
LINEAR_ATTN_HEAD = 32
DH = 128
STRETCH = 128
LIN_DEV = 512
PREFILL_SPAN = 16384


def query_exponents(key):
    return jax.random.randint(jax.random.fold_in(key, 21), (PREFILL_SPAN, HS), -1, 2).astype(jnp.int32)


def key_exponents(key):
    return jax.random.randint(jax.random.fold_in(key, 22), (PREFILL_SPAN, HS), -1, 2).astype(jnp.int32)


def draw_q_exps(key, part):
    return query_exponents(key)


def draw_k_exps(key, part):
    return key_exponents(key)


def draw_q_codes(key, part):
    key = jax.random.fold_in(key, 1)
    code_values = jnp.clip(jax.random.normal(key, (PREFILL_SPAN, HS, DH), jnp.float32), -6.0, 6.0)
    return code_values.reshape(PREFILL_SPAN, HS * DH).astype(jnp.bfloat16)


def draw_k_codes(key, part):
    key = jax.random.fold_in(key, 2)
    code_values = jnp.clip(jax.random.normal(key, (PREFILL_SPAN, HS, DH), jnp.float32), -6.0, 6.0)
    return code_values.reshape(PREFILL_SPAN, HS * DH).astype(jnp.bfloat16)


def draw_decay_log(key, part):
    key = jax.random.fold_in(key, 7)
    lookup_ordering = jax.random.split(key, 7)
    fast_share = 0.5
    quick_heads = jax.random.uniform(lookup_ordering[0], (LINEAR_ATTN_HEAD,), jnp.float32) < fast_share
    quick_rate = jnp.exp(jax.random.uniform(lookup_ordering[1], (LINEAR_ATTN_HEAD,), jnp.float32, math.log(1.0 / 50.0), math.log(1.0 / 30.0)))
    slow_rate = jnp.exp(jax.random.uniform(lookup_ordering[2], (LINEAR_ATTN_HEAD,), jnp.float32, math.log(0.1), math.log(0.6))) / PREFILL_SPAN
    base_rate = jnp.where(quick_heads, quick_rate, slow_rate)
    blocks = jnp.exp(jax.random.uniform(lookup_ordering[3], (PREFILL_SPAN // LIN_DEV, 1), jnp.float32, math.log(0.5), math.log(2.0)))
    block_factor = jnp.repeat(blocks, LIN_DEV, axis=0)
    roughness = jax.random.uniform(lookup_ordering[4], (PREFILL_SPAN, LINEAR_ATTN_HEAD), jnp.float32, 0.5, 1.5)
    forget_ratio = -base_rate[None, :] * block_factor * roughness
    segment_groups = jax.random.uniform(lookup_ordering[5], (PREFILL_SPAN, LINEAR_ATTN_HEAD), jnp.float32) < 3.0 / PREFILL_SPAN
    segment_span = jax.random.uniform(lookup_ordering[6], (PREFILL_SPAN, LINEAR_ATTN_HEAD), jnp.float32, math.log(0.5), math.log(0.8))
    return jnp.where(segment_groups, forget_ratio + segment_span, forget_ratio).astype(jnp.float32)


def plant(values, stream_key, least, top_value):
    place = [jax.random.randint(jax.random.fold_in(stream_key, axis), (), 0, length) for axis, length in enumerate(values.shape)]
    widest = values.shape.index(max(values.shape))
    beside = place[:widest] + [(place[widest] + 1) % values.shape[widest]] + place[widest + 1:]
    return values.at[tuple(place)].set(least).at[tuple(beside)].set(top_value)


def levels(key, shape, cuts, least, high):
    loudness, own = 1.0, jax.random.fold_in(key, 6)
    for position, parts in cuts:
        steps = jnp.exp(jax.random.uniform(jax.random.fold_in(own, position), (parts,), jnp.float32, least / len(cuts), high / len(cuts)))
        loudness = loudness * jnp.repeat(steps, shape[position] // parts).reshape([-1 if axis == position else 1 for axis in range(len(shape))])
    return loudness


def centred(rng, extent, width, most, cuts=(), held_as=jnp.bfloat16):
    entries = jax.random.normal(rng, extent, jnp.float32) * width
    if len(cuts) > 0:
        entries = levels(rng, extent, cuts, -0.22, 0.18) * entries
    return jnp.clip(entries, min=-most, max=most).astype(held_as)


def setup_inputs(seed: int = 0) -> dict:
    arg_keys = jax.random.split(jax.random.key(seed), 11)
    q_codes = draw_q_codes(jax.random.fold_in(arg_keys[10], 71), 0)
    q_exps = draw_q_exps(jax.random.fold_in(arg_keys[10], 71), 0)
    k_codes = draw_k_codes(jax.random.fold_in(arg_keys[10], 71), 0)
    k_exps = draw_k_exps(jax.random.fold_in(arg_keys[10], 71), 0)
    v_codes = centred(arg_keys[4], (PREFILL_SPAN, HS * DH), 1.0, 6.0, ((0, 256),))
    v_exps = plant(jax.random.randint(arg_keys[5], (PREFILL_SPAN, HS), -1, 2), jax.random.fold_in(arg_keys[5], 1), -1, 1).astype(jnp.int32)
    lin_query = centred(arg_keys[6], (PREFILL_SPAN, LINEAR_ATTN_HEAD * DH), 1.0, 6.0, ((0, 32), (1, 8)))
    lin_keys = centred(arg_keys[7], (PREFILL_SPAN, LINEAR_ATTN_HEAD * DH), 1.0, 6.0, ((0, 32), (1, 8)))
    lin_values = centred(arg_keys[8], (PREFILL_SPAN, LINEAR_ATTN_HEAD * DH), 1.0, 6.0, ((0, 32), (1, 8)))
    decay_log = draw_decay_log(jax.random.fold_in(arg_keys[10], 71), 0)
    return dict(q_codes=q_codes, q_exps=q_exps, k_codes=k_codes, k_exps=k_exps, v_codes=v_codes, v_exps=v_exps, lin_query=lin_query, lin_keys=lin_keys, lin_values=lin_values, decay_log=decay_log)


def dequantize(code_rows, exponents):
    head_total = exponents.shape[1]
    scaled = code_rows.reshape(code_rows.shape[0], head_total, -1).astype(jnp.float32)
    scaled = scaled * jnp.exp2(exponents.astype(jnp.float32))[:, :, None]
    return scaled.astype(jnp.bfloat16)

def softmax_layer(queries, key_data, value_data):
    block_rows = 512 if PREFILL_SPAN % 512 == 0 else PREFILL_SPAN
    block_count = PREFILL_SPAN // block_rows
    positions = jnp.arange(PREFILL_SPAN, dtype=jnp.int32)
    score_scale = DH ** (-0.5)

    def one_head(operand):
        query_head, key_head, value_head = operand

        def one_block(pieces):
            query_block, query_pos = pieces
            scores = jnp.dot(query_block, key_head.T, preferred_element_type=jnp.float32) * score_scale
            visible = positions[None, :] <= query_pos[:, None]
            scores = jnp.where(visible, scores, -jnp.inf)
            row_max = lax.optimization_barrier(jnp.max(scores, axis=1, keepdims=True))
            raw_weights = jnp.where(visible, jnp.exp(scores - row_max), 0.0)
            row_sum = lax.optimization_barrier(jnp.sum(raw_weights, axis=1, keepdims=True))
            weighted = jnp.dot(raw_weights.astype(jnp.bfloat16), value_head, preferred_element_type=jnp.float32)
            return (weighted / row_sum).astype(jnp.bfloat16)
        return lax.map(one_block, (query_head.reshape(block_count, block_rows, DH), positions.reshape(block_count, block_rows)))
    result = lax.map(one_head, (jnp.transpose(queries, (1, 0, 2)), jnp.transpose(key_data, (1, 0, 2)), jnp.transpose(value_data, (1, 0, 2))))
    result = result.reshape(HS, PREFILL_SPAN, DH)
    return jnp.transpose(result, (1, 0, 2)).reshape(PREFILL_SPAN, HS * DH)

def lightning_layer(lin_query, lin_keys, lin_values, decay_log):
    block_count = PREFILL_SPAN // STRETCH
    query_tiles_list = lin_query.reshape(block_count, STRETCH, LINEAR_ATTN_HEAD, DH)
    lookup_segments = lin_keys.reshape(block_count, STRETCH, LINEAR_ATTN_HEAD, DH)
    value_blocks = lin_values.reshape(block_count, STRETCH, LINEAR_ATTN_HEAD, DH)
    decay_blocks = decay_log.reshape(block_count, STRETCH, LINEAR_ATTN_HEAD)
    causal = jnp.tril(jnp.ones((STRETCH, STRETCH), dtype=bool))[None]

    def one_block(carried, operand):
        query_block, key_block, value_block, decay_block = operand
        log_cum = jnp.cumsum(decay_block, axis=0)
        log_last = log_cum[-1]
        scores = jnp.einsum('qhd,khd->hqk', query_block.astype(jnp.float32), key_block.astype(jnp.float32))
        cum_heads = log_cum.T
        log_gap = cum_heads[:, :, None] - cum_heads[:, None, :]
        block_weights = jnp.where(causal, scores * jnp.exp(jnp.where(causal, log_gap, 0.0)), 0.0).astype(jnp.bfloat16)
        inner_part = jnp.einsum('hqk,khd->qhd', block_weights.astype(jnp.float32), value_block.astype(jnp.float32))
        query_decayed = (query_block.astype(jnp.float32) * jnp.exp(log_cum)[:, :, None]).astype(jnp.bfloat16)
        key_decayed = (key_block.astype(jnp.float32) * jnp.exp(log_last[None, :] - log_cum)[:, :, None]).astype(jnp.bfloat16)
        state_bf = carried.astype(jnp.bfloat16)
        outer_part = jnp.einsum('qhd,hde->qhe', query_decayed.astype(jnp.float32), state_bf.astype(jnp.float32))
        update = jnp.einsum('khd,khe->hde', key_decayed.astype(jnp.float32), value_block.astype(jnp.float32))
        new_state = jnp.exp(log_last)[:, None, None] * carried + update
        mixed_rows = inner_part + outer_part
        rms_value = jnp.sqrt(lax.optimization_barrier(jnp.mean(mixed_rows * mixed_rows, axis=2, keepdims=True)) + 1e-06)
        return (new_state, (mixed_rows / rms_value).astype(jnp.bfloat16))
    initial = jnp.zeros((LINEAR_ATTN_HEAD, DH, DH), dtype=jnp.float32)
    _, outputs = lax.scan(one_block, initial, (query_tiles_list, lookup_segments, value_blocks, decay_blocks))
    return outputs.reshape(PREFILL_SPAN, LINEAR_ATTN_HEAD * DH)

def reference(q_codes, q_exps, k_codes, k_exps, v_codes, v_exps, lin_query, lin_keys, lin_values, decay_log):
    queries = dequantize(q_codes, q_exps)
    key_data = dequantize(k_codes, k_exps)
    value_data = dequantize(v_codes, v_exps)
    soft_out = softmax_layer(queries, key_data, value_data)
    lin_out = lightning_layer(lin_query, lin_keys, lin_values, decay_log)
    return (soft_out, lin_out)
```

```python
import math

import jax
import jax.numpy as jnp
from jax import lax
from jax.experimental import pallas as pl
from jax.experimental.pallas import tpu as pltpu
from jax.sharding import PartitionSpec as P

STRETCH = 128
TILE = 256
HIDDEN = -1e30
VMEM = pl.BlockSpec(memory_space=pltpu.VMEM)
SMEM = pl.BlockSpec(memory_space=pltpu.SMEM)
ANY = pl.BlockSpec(memory_space=pl.ANY)


def limits(megabytes):
    return pltpu.CompilerParams(vmem_limit_bytes=megabytes * 1024 * 1024)


def shifted(value, axis, steps):
    count = lax.axis_size(axis)
    pairs = [(i, i + steps) for i in range(count) if 0 <= i + steps < count]
    return lax.ppermute(value, axis, pairs)


def ring(value, steps):
    count = lax.axis_size("head")
    return lax.ppermute(value, "head", [(i, (i + steps) % count) for i in range(count)])


def core_swap(value):
    count = lax.axis_size("head")
    return lax.ppermute(value, "head", [(i, i ^ 1) for i in range(count)])


def prepare(codes, exponents):
    tokens, heads = exponents[0].shape
    width = codes[0].shape[1] // heads

    def kernel(*refs):
        out = refs[-1]
        for n in range(3):
            scale = jnp.exp2(refs[3 + n][...].astype(jnp.float32))
            for h in range(heads):
                rows = refs[n][:, h * width : (h + 1) * width].astype(jnp.float32)
                rows = rows * scale[:, h : h + 1]
                out[h, n * tokens : (n + 1) * tokens, :] = rows.astype(jnp.bfloat16)

    return pl.pallas_call(
        kernel,
        in_specs=[VMEM] * 6,
        out_specs=VMEM,
        out_shape=jax.ShapeDtypeStruct((heads, 3 * tokens, width), jnp.bfloat16),
        compiler_params=limits(16),
    )(*codes, *exponents)


def attend(ranks, query, chunks, state, finish=False):
    seq_count, key_dev, head_dim = query.shape
    rows = seq_count * key_dev
    span = key_dev * lax.axis_size("head")
    per = TILE // key_dev
    tiles = rows // TILE
    chunk_count = len(chunks)
    pairs = chunk_count // 2
    pieces = [(n, piece) for n, chunk in enumerate(chunks) for piece in chunk]
    scale = math.log2(math.e) / math.sqrt(head_dim)
    first = state is None

    def kernel(*refs):
        refs = list(refs)
        ranks_ref, q_ref = refs.pop(0), refs.pop(0)
        sources = [refs.pop(0) for _ in pieces]
        given = [] if first else [refs.pop(0) for _ in range(3)]
        o_ref = refs.pop(0) if finish else None
        m_ref, l_ref, acc_ref, held, sems, score_a, score_b = refs
        copies = [[] for _ in chunks]
        filled = [0] * chunk_count
        for at, (n, piece) in enumerate(pieces):
            extent = piece.shape[0]
            target = held.at[n, pl.ds(filled[n], extent)]
            copies[n].append(pltpu.make_async_copy(sources[at], target, sems.at[at]))
            filled[n] += extent
        for n in range(chunk_count):
            for copy in copies[n]:
                copy.start()
        if first:
            m_ref[...] = jnp.full_like(m_ref, HIDDEN)
            l_ref[...] = jnp.zeros_like(l_ref)
            acc_ref[...] = jnp.zeros_like(acc_ref)
        else:
            m_ref[...] = given[0][...]
            l_ref[...] = given[1][...]
            acc_ref[...] = given[2][...]
        own = ranks_ref[0]
        score_refs = (score_a, score_b)

        def units(i):
            return [(c, j) for c in range(2) for j in range(i + 1)]

        def one_pair(p):
            def produce(i, n, unit, q, top):
                c, j = unit
                keys = held[2 * p + c, j * per : (j + 1) * per, :key_dev, :].reshape(TILE, head_dim)
                s = lax.dot_general(
                    keys, q, (((1,), (1,)), ((), ())), preferred_element_type=jnp.float32
                )
                if j == i:
                    a = lax.broadcasted_iota(jnp.int32, (TILE, TILE), 0)
                    b = lax.broadcasted_iota(jnp.int32, (TILE, TILE), 1)
                    key_pos = a // key_dev * span + ranks_ref[1 + 2 * p + c] * key_dev + a % key_dev
                    query_pos = b // key_dev * span + own * key_dev + b % key_dev
                    s = jnp.where(key_pos <= query_pos, s, HIDDEN)
                score_refs[i % 2][n * TILE : (n + 1) * TILE, :] = s
                part = jnp.max(s.reshape(TILE // 8, 8, TILE), axis=0)
                return part if top is None else jnp.maximum(top, part)

            def consume(i, n, unit, offset, total, weighted):
                c, j = unit
                s = score_refs[i % 2][n * TILE : (n + 1) * TILE, :]
                w = jnp.exp2(s * scale - offset)
                values = held[2 * p + c, j * per : (j + 1) * per, key_dev:, :].reshape(
                    TILE, head_dim
                )
                x = lax.dot_general(
                    values,
                    w.astype(jnp.bfloat16),
                    (((0,), (0,)), ((), ())),
                    preferred_element_type=jnp.float32,
                )
                part = jnp.sum(w.reshape(TILE // 8, 8, TILE), axis=0)
                if total is None:
                    return part, x
                return total + part, weighted + x

            before = None
            for i in [*range(tiles), None]:
                ahead = [] if i is None else units(i)
                if i is not None:
                    q = q_ref[i * per : (i + 1) * per].reshape(TILE, head_dim)
                behind = []
                if before is not None:
                    done, top = before
                    cols = slice(done * TILE, (done + 1) * TILE)
                    old = m_ref[done : done + 1, :]
                    new = jnp.maximum(old, jnp.max(top, axis=0, keepdims=True))
                    m_ref[done : done + 1, :] = new
                    fade = jnp.exp2((old - new) * scale)
                    offset = new * scale
                    behind = units(done)
                top = total = weighted = None
                a = b = 0
                while a < len(ahead) or b < len(behind):
                    if a < len(ahead) and (
                        b >= len(behind) or a * len(behind) <= b * len(ahead)
                    ):
                        top = produce(i, a, ahead[a], q, top)
                        a += 1
                    else:
                        total, weighted = consume(done, b, behind[b], offset, total, weighted)
                        b += 1
                if before is not None:
                    l_ref[done : done + 1, :] = l_ref[done : done + 1, :] * fade + jnp.sum(
                        total, axis=0, keepdims=True
                    )
                    acc_ref[:, cols] = acc_ref[:, cols] * fade + weighted
                before = (i, top)

        if pairs == 1:
            for n in range(chunk_count):
                for copy in copies[n]:
                    copy.wait()
            one_pair(0)
        else:

            def step(p, unused):
                for n in range(chunk_count):

                    @pl.when(p == n // 2)
                    def _(n=n):
                        for copy in copies[n]:
                            copy.wait()

                one_pair(p)
                return unused

            lax.fori_loop(0, pairs, step, 0)
        if finish:
            for i in range(tiles):
                cols = slice(i * TILE, (i + 1) * TILE)
                o = (acc_ref[:, cols] / l_ref[i : i + 1, :]).T.astype(jnp.bfloat16)
                o_ref[i * per : (i + 1) * per] = o.reshape(per, key_dev, head_dim)

    state_shape = [
        jax.ShapeDtypeStruct((tiles, TILE), jnp.float32),
        jax.ShapeDtypeStruct((tiles, TILE), jnp.float32),
        jax.ShapeDtypeStruct((head_dim, rows), jnp.float32),
    ]
    scratch = [
        pltpu.VMEM((chunk_count, seq_count, 2 * key_dev, head_dim), jnp.bfloat16),
        pltpu.SemaphoreType.DMA((len(pieces),)),
        pltpu.VMEM((2 * rows, TILE), jnp.float32),
        pltpu.VMEM((2 * rows, TILE), jnp.float32),
    ]
    if finish:
        out_shape, out_specs = jax.ShapeDtypeStruct(query.shape, jnp.bfloat16), VMEM
        scratch = [pltpu.VMEM(s.shape, s.dtype) for s in state_shape] + scratch
    else:
        out_shape, out_specs = state_shape, [VMEM] * 3
    flops = chunk_count * rows * rows * head_dim * 2
    return pl.pallas_call(
        kernel,
        in_specs=[SMEM, VMEM] + [ANY] * len(pieces) + ([] if first else [VMEM] * 3),
        out_specs=out_specs,
        out_shape=out_shape,
        scratch_shapes=scratch,
        cost_estimate=pl.CostEstimate(
            flops=flops, bytes_accessed=(chunk_count + 2) * 2**20, transcendentals=flops // 512
        ),
        compiler_params=limits(32),
    )(ranks, query, *[piece for _, piece in pieces], *([] if first else state))


def softmax_layer(q_codes, q_exps, k_codes, k_exps, v_codes, v_exps):
    rank = lax.axis_index("head")
    count = lax.axis_size("head")
    tokens = q_codes.shape[0]
    packed = prepare((k_codes, v_codes, q_codes), (k_exps, v_exps, q_exps))
    packed = lax.all_to_all(packed, "seq", split_axis=0, concat_axis=0, tiled=True)
    half = packed.shape[0] // 2
    query = packed[:, 2 * tokens :]
    own = packed[:, : 2 * tokens]
    partner = core_swap(own)
    below = ring(own, 2)
    above = ring(own, -2)
    far_low = ring(below[:half], 2)
    far_high = ring(above[half:], -2)
    below_other = core_swap(below)
    above_other = core_swap(above)
    far_low_other = core_swap(far_low)
    far_high_other = core_swap(far_high)

    def ranks(*steps):
        chip, core = rank // 2, rank % 2
        listed = [rank]
        for chips, cores in steps:
            listed.append((chip + chips) % (count // 2) * 2 + (core + cores) % 2)
        return jnp.stack(listed).astype(jnp.int32)

    state = attend(ranks((0, 0), (0, 1)), query, [[own], [partner]], None)
    state = attend(
        ranks((-1, 0), (-1, 1), (1, 0), (1, 1)),
        query,
        [[below], [below_other], [above], [above_other]],
        state,
    )
    attended = attend(
        ranks((2, 0), (2, 1)),
        query,
        [[far_low, far_high], [far_low_other, far_high_other]],
        state,
        finish=True,
    )
    mine = lax.all_to_all(attended, "seq", split_axis=0, concat_axis=0, tiled=True)
    return jnp.swapaxes(mine, 0, 1).reshape(tokens, -1)


def lightning_update(keys, values, cum, last):
    rows, width = keys.shape
    heads = cum.shape[1]
    head_dim = width // heads

    def kernel(k_ref, v_ref, cum_ref, last_ref, out_ref):
        for h in range(heads):
            cols = slice(h * head_dim, (h + 1) * head_dim)
            state = jnp.zeros((head_dim, head_dim), jnp.float32)
            for b in range(rows // STRETCH):
                span = slice(b * STRETCH, (b + 1) * STRETCH)
                end = last_ref[b : b + 1, h : h + 1]
                decayed = k_ref[span, cols].astype(jnp.float32) * jnp.exp(
                    end - cum_ref[span, h : h + 1]
                )
                update = lax.dot_general(
                    decayed.astype(jnp.bfloat16),
                    v_ref[span, cols],
                    (((0,), (0,)), ((), ())),
                    preferred_element_type=jnp.float32,
                )
                state = jnp.exp(end) * state + update
            out_ref[h] = state

    return pl.pallas_call(
        kernel,
        in_specs=[VMEM] * 4,
        out_specs=VMEM,
        out_shape=jax.ShapeDtypeStruct((heads, head_dim, head_dim), jnp.float32),
        compiler_params=limits(16),
    )(keys, values, cum, last)


def lightning_output(query, keys, values, cum, cum_rows, last, entering):
    rows, width = keys.shape
    heads = cum.shape[1]
    head_dim = width // heads
    blocks = rows // STRETCH

    def kernel(q_ref, k_ref, v_ref, cum_ref, row_ref, last_ref, state_ref, out_ref):
        a = lax.broadcasted_iota(jnp.int32, (STRETCH, STRETCH), 0)
        b = lax.broadcasted_iota(jnp.int32, (STRETCH, STRETCH), 1)
        causal = b <= a
        for h in range(heads):
            cols = slice(h * head_dim, (h + 1) * head_dim)
            state = state_ref[h]
            for n in range(blocks):
                span = slice(n * STRETCH, (n + 1) * STRETCH)
                q, k, v = q_ref[span, cols], k_ref[span, cols], v_ref[span, cols]
                here = cum_ref[span, h : h + 1]
                scores = lax.dot_general(
                    q, k, (((1,), (1,)), ((), ())), preferred_element_type=jnp.float32
                )
                gap = jnp.where(causal, here - row_ref[h : h + 1, span], 0.0)
                weights = jnp.where(causal, scores * jnp.exp(gap), 0.0).astype(jnp.bfloat16)
                mixed = jnp.dot(weights, v, preferred_element_type=jnp.float32)
                decayed = (q.astype(jnp.float32) * jnp.exp(here)).astype(jnp.bfloat16)
                mixed += jnp.dot(
                    decayed, state.astype(jnp.bfloat16), preferred_element_type=jnp.float32
                )
                mean = jnp.mean(mixed * mixed, axis=1, keepdims=True)
                out_ref[span, cols] = (mixed / jnp.sqrt(mean + 1e-06)).astype(jnp.bfloat16)
                if n < blocks - 1:
                    end = last_ref[n : n + 1, h : h + 1]
                    aged = (k.astype(jnp.float32) * jnp.exp(end - here)).astype(jnp.bfloat16)
                    state = jnp.exp(end) * state + lax.dot_general(
                        aged, v, (((0,), (0,)), ((), ())), preferred_element_type=jnp.float32
                    )

    return pl.pallas_call(
        kernel,
        in_specs=[VMEM] * 7,
        out_specs=VMEM,
        out_shape=jax.ShapeDtypeStruct((rows, width), jnp.bfloat16),
        compiler_params=limits(16),
    )(query, keys, values, cum, cum_rows, last, entering)


def entering_state(state, log_fade):
    heads, head_dim, _ = state.shape

    def sent(value, log_value, steps):
        high = log_value.astype(jnp.bfloat16)
        rest = log_value - high.astype(jnp.float32)
        mid = rest.astype(jnp.bfloat16)
        low = (rest - mid.astype(jnp.float32)).astype(jnp.bfloat16)
        parts = jnp.stack([high, mid, low], axis=1)
        parts = jnp.pad(parts, ((0, 0), (0, 13)))
        parts = jnp.broadcast_to(parts[:, :, None], (heads, 16, head_dim))
        message = jnp.concatenate([value.astype(jnp.bfloat16), parts], axis=1)
        message = shifted(message, "seq", steps).astype(jnp.float32)
        return message[:, :head_dim], jnp.sum(message[:, head_dim : head_dim + 3, 0], axis=1)

    value, log_value = sent(state, log_fade, 1)
    steps = 1
    while steps < lax.axis_size("seq"):
        other, log_other = sent(value, log_value, steps)
        value = value + jnp.exp(log_value)[:, None, None] * other
        log_value = log_value + log_other
        steps *= 2
    return value


def lightning_layer(lin_query, lin_keys, lin_values, decay_log):
    rows, heads = decay_log.shape
    cum = jnp.cumsum(decay_log.reshape(rows // STRETCH, STRETCH, heads), axis=1)
    last = cum[:, -1]
    cum = cum.reshape(rows, heads)
    state = lightning_update(lin_keys, lin_values, cum, last)
    entering = entering_state(state, jnp.sum(last, axis=0))
    return lightning_output(lin_query, lin_keys, lin_values, cum, cum.T, last, entering)


def shards(
    q_codes, q_exps, k_codes, k_exps, v_codes, v_exps, lin_query, lin_keys, lin_values, decay_log
):
    soft_out = softmax_layer(q_codes, q_exps, k_codes, k_exps, v_codes, v_exps)
    lin_out = lightning_layer(lin_query, lin_keys, lin_values, decay_log)
    return (soft_out, lin_out)


def solution(mesh):
    rows = P(("seq", "head"), None)
    tiles = P("seq", "head")
    return jax.shard_map(
        shards,
        mesh=mesh,
        in_specs=(rows,) * 6 + (tiles,) * 4,
        out_specs=(rows, tiles),
        check_vma=False,
    )
```

```python
import math

import jax
import jax.numpy as jnp
from jax import lax
from jax.experimental import pallas as pl
from jax.experimental.pallas import tpu as pltpu
from jax.sharding import PartitionSpec as P

STRETCH = 128
TILE = 256
HIDDEN = -1e30
VMEM = pl.BlockSpec(memory_space=pltpu.VMEM)
SMEM = pl.BlockSpec(memory_space=pltpu.SMEM)
ANY = pl.BlockSpec(memory_space=pl.ANY)
WHOLE = pl.BlockSpec()


def limits(megabytes):
    return pltpu.CompilerParams(vmem_limit_bytes=megabytes * 1024 * 1024)


def ring(value, steps):
    count = lax.axis_size("head")
    return lax.ppermute(value, "head", [(i, (i + steps) % count) for i in range(count)])


def core_swap(value):
    count = lax.axis_size("head")
    return lax.ppermute(value, "head", [(i, i ^ 1) for i in range(count)])


def after(value, *others):
    return lax.optimization_barrier((value, *others))[0]


def prepare(codes, exponents):
    heads, tokens = exponents[0].shape
    width = codes[0].shape[1] // heads
    count = len(codes)

    def kernel(*refs):
        out = refs[-1]
        for n in range(count):
            scale = jnp.exp2(refs[count + n][...].astype(jnp.float32)).T
            for h in range(heads):
                rows = refs[n][:, h * width : (h + 1) * width].astype(jnp.float32)
                rows = rows * scale[:, h : h + 1]
                out[h, n * tokens : (n + 1) * tokens, :] = rows.astype(jnp.bfloat16)

    return pl.pallas_call(
        kernel,
        in_specs=[WHOLE] * (2 * count),
        out_specs=VMEM,
        out_shape=jax.ShapeDtypeStruct((heads, count * tokens, width), jnp.bfloat16),
        compiler_params=limits(60),
    )(*codes, *exponents)


def attend(ranks, query, chunks, state, span, tail=None):
    seq_count, key_dev, head_dim = chunks[0].shape
    key_dev //= 2
    finish = tail is not None
    rows = seq_count * key_dev
    per = TILE // key_dev
    tiles = rows // TILE
    order = [*range(0, tiles, 2), *range(tiles - 1, 0, -2)]
    early = (max(order[:2]) + 1) * per
    chunk_count = len(chunks)
    pairs = chunk_count // 2
    scale = math.log2(math.e) / math.sqrt(head_dim)
    first = state is None

    def kernel(*refs):
        refs = list(refs)
        ranks_ref, q_ref = refs.pop(0), refs.pop(0)
        sources = [refs.pop(0) for _ in chunks]
        given = [] if first else [refs.pop(0) for _ in range(3)]
        tail_ref = refs.pop(0) if finish else None
        o_ref = refs.pop(0) if finish else None
        m_ref, l_ref, acc_ref, held, sems, score_a, score_b = refs
        score_refs = (score_a, score_b)
        parts = (slice(0, early), slice(early, seq_count))
        copies = [
            [
                pltpu.make_async_copy(sources[n].at[part], held.at[n, part], sems.at[n, m])
                for n in range(chunk_count)
            ]
            for m, part in enumerate(parts)
        ]
        for copy in copies[0] + copies[1]:
            copy.start()
        if finish:
            o_ref[:, key_dev:, :] = tail_ref[...]
        if first:
            m_ref[...] = jnp.full_like(m_ref, HIDDEN)
            l_ref[...] = jnp.zeros_like(l_ref)
            acc_ref[...] = jnp.zeros_like(acc_ref)
        else:
            m_ref[...] = given[0][...]
            l_ref[...] = given[1][...]
            acc_ref[...] = given[2][...]
        own = ranks_ref[0]

        def units(i):
            return [(c, j) for c in range(2) for j in range(i + 1)]

        def produce(p, slot, i, n, q, top):
            c, j = units(i)[n]
            keys = held[2 * p + c, j * per : (j + 1) * per, :key_dev, :].reshape(TILE, head_dim)
            s = lax.dot_general(
                keys, q, (((1,), (1,)), ((), ())), preferred_element_type=jnp.float32
            )
            if j == i:
                a = lax.broadcasted_iota(jnp.int32, (TILE, TILE), 0)
                b = lax.broadcasted_iota(jnp.int32, (TILE, TILE), 1)
                key_pos = a // key_dev * span + ranks_ref[1 + 2 * p + c] * key_dev + a % key_dev
                query_pos = b // key_dev * span + own * key_dev + b % key_dev
                s = jnp.where(key_pos <= query_pos, s, HIDDEN)
            score_refs[slot][n * TILE : (n + 1) * TILE, :] = s
            part = jnp.max(s.reshape(TILE // 8, 8, TILE), axis=0)
            return part if top is None else jnp.maximum(top, part)

        def consume(p, slot, i, n, offset, total, weighted):
            c, j = units(i)[n]
            s = score_refs[slot][n * TILE : (n + 1) * TILE, :]
            w = jnp.exp2(s * scale - offset)
            values = held[2 * p + c, j * per : (j + 1) * per, key_dev:, :].reshape(TILE, head_dim)
            x = lax.dot_general(
                values,
                w.astype(jnp.bfloat16),
                (((0,), (0,)), ((), ())),
                preferred_element_type=jnp.float32,
            )
            part = jnp.sum(w.reshape(TILE // 8, 8, TILE), axis=0)
            if total is None:
                return part, x
            return total + part, weighted + x

        def stage(p, at, before):
            i = order[at] if at < tiles else None
            done = order[at - 1] if at > 0 else None
            here, there = at % 2, (at + 1) % 2
            ahead = behind = 0
            if i is not None:
                q = q_ref[i * per : (i + 1) * per, :key_dev, :].reshape(TILE, head_dim)
                ahead = len(units(i))
            if done is not None:
                cols = slice(done * TILE, (done + 1) * TILE)
                old = m_ref[done : done + 1, :]
                new = jnp.maximum(old, jnp.max(before, axis=0, keepdims=True))
                m_ref[done : done + 1, :] = new
                fade = jnp.exp2((old - new) * scale)
                offset = new * scale
                behind = len(units(done))
            top = total = weighted = None
            a = b = 0
            while a < ahead or b < behind:
                if a < ahead and (b >= behind or a * behind <= b * ahead):
                    top = produce(p, here, i, a, q, top)
                    a += 1
                else:
                    total, weighted = consume(p, there, done, b, offset, total, weighted)
                    b += 1
            if done is not None:
                total = l_ref[done : done + 1, :] * fade + jnp.sum(total, axis=0, keepdims=True)
                weighted = acc_ref[:, cols] * fade + weighted
                if finish:
                    o = (weighted / total).T.astype(jnp.bfloat16).reshape(per, key_dev, head_dim)
                    o_ref[done * per : (done + 1) * per, :key_dev, :] = o
                else:
                    l_ref[done : done + 1, :] = total
                    acc_ref[:, cols] = weighted

            @pl.when(own < 0)
            def _():
                m_ref[0:1, :] = jnp.zeros((1, TILE), jnp.float32)

            return top

        def step(p, unused):
            def arrive(m):
                for n in range(chunk_count):

                    @pl.when(p == n // 2)
                    def _(n=n):
                        copies[m][n].wait()

            arrive(0)
            top = None
            for at in range(tiles + 1):
                if at == 2:
                    arrive(1)
                top = stage(p, at, top)
            return unused

        lax.fori_loop(0, pairs, step, 0)

    state_shape = [
        jax.ShapeDtypeStruct((tiles, TILE), jnp.float32),
        jax.ShapeDtypeStruct((tiles, TILE), jnp.float32),
        jax.ShapeDtypeStruct((head_dim, rows), jnp.float32),
    ]
    scratch = [
        pltpu.VMEM((chunk_count, seq_count, 2 * key_dev, head_dim), jnp.bfloat16),
        pltpu.SemaphoreType.DMA((chunk_count, 2)),
        pltpu.VMEM((2 * rows, TILE), jnp.float32),
        pltpu.VMEM((2 * rows, TILE), jnp.float32),
    ]
    if finish:
        out_rows = key_dev + tail.shape[1]
        out_shape = jax.ShapeDtypeStruct((seq_count, out_rows, head_dim), jnp.bfloat16)
        out_specs = VMEM
        scratch = [pltpu.VMEM(s.shape, s.dtype) for s in state_shape] + scratch
    else:
        out_shape, out_specs = state_shape, [VMEM] * 3
    extra = ([] if first else [*state]) + ([tail] if finish else [])
    flops = 2 * chunk_count * rows * rows * head_dim * 2
    return pl.pallas_call(
        kernel,
        in_specs=[SMEM, VMEM] + [ANY] * chunk_count + [VMEM] * len(extra),
        out_specs=out_specs,
        out_shape=out_shape,
        scratch_shapes=scratch,
        cost_estimate=pl.CostEstimate(
            flops=flops, bytes_accessed=(chunk_count + 2) * 2**20, transcendentals=flops // 1024
        ),
        compiler_params=limits(20),
    )(ranks, query, *chunks, *extra)


def summed(decay):
    tokens = decay.shape[1]
    a = lax.broadcasted_iota(jnp.int32, (tokens, tokens), 0)
    b = lax.broadcasted_iota(jnp.int32, (tokens, tokens), 1)
    ones = jnp.where(a <= b, 1.0, 0.0).astype(jnp.float32)
    cum = jnp.dot(
        decay, ones, precision=lax.Precision.HIGHEST, preferred_element_type=jnp.float32
    )
    return cum, cum.T


def prepare_rest(codes, exponents, query, keys, values, decay_rows, seq_count):
    soft_heads, tokens = exponents.shape
    width = codes.shape[1] // soft_heads
    rows = keys.shape[0]
    heads = decay_rows.shape[0]
    head_dim = keys.shape[1] // heads
    blocks = rows // STRETCH
    shares = seq_count // heads
    share = head_dim // shares

    def kernel(code_ref, exps_ref, q_ref, k_ref, v_ref, decay_ref, *out):
        packed_ref, inner_ref, decayed_ref, before_ref, fade_ref = out
        scale = jnp.exp2(exps_ref[...].astype(jnp.float32)).T
        for h in range(soft_heads):
            part = code_ref[:, h * width : (h + 1) * width].astype(jnp.float32)
            packed_ref[h, :tokens, :] = (part * scale[:, h : h + 1]).astype(jnp.bfloat16)
        a = lax.broadcasted_iota(jnp.int32, (STRETCH, STRETCH), 0)
        b = lax.broadcasted_iota(jnp.int32, (STRETCH, STRETCH), 1)
        causal = b <= a
        place = lax.broadcasted_iota(jnp.int32, (share, head_dim), 0)
        states = [jnp.zeros((head_dim, head_dim), jnp.float32)] * heads
        log_total = jnp.zeros((heads, 1), jnp.float32)
        for n in range(blocks):
            span = slice(n * STRETCH, (n + 1) * STRETCH)
            cum, cum_cols = summed(decay_ref[:, span])
            for h in range(heads):
                cols = slice(h * head_dim, (h + 1) * head_dim)
                q, k, v = q_ref[span, cols], k_ref[span, cols], v_ref[span, cols]
                here, end = cum_cols[:, h : h + 1], cum[h : h + 1, STRETCH - 1 : STRETCH]
                scores = lax.dot_general(
                    q, k, (((1,), (1,)), ((), ())), preferred_element_type=jnp.float32
                )
                gap = jnp.where(causal, here - cum[h : h + 1], 0.0)
                weights = jnp.where(causal, scores * jnp.exp(gap), 0.0).astype(jnp.bfloat16)
                inner_ref[span, cols] = jnp.dot(weights, v, preferred_element_type=jnp.float32)
                decayed = (q.astype(jnp.float32) * jnp.exp(here)).astype(jnp.bfloat16)
                decayed_ref[span, cols] = decayed
                before_ref[n, h] = states[h]
                fade = jnp.exp(log_total[h : h + 1])
                fade_ref[n * heads + h : n * heads + h + 1, :] = jnp.broadcast_to(
                    fade, (1, head_dim)
                )
                aged = (k.astype(jnp.float32) * jnp.exp(end - here)).astype(jnp.bfloat16)
                states[h] = jnp.exp(end) * states[h] + lax.dot_general(
                    aged, v, (((0,), (0,)), ((), ())), preferred_element_type=jnp.float32
                )
            log_total += cum[:, STRETCH - 1 : STRETCH]
        for h in range(heads):
            log = jnp.broadcast_to(log_total[h : h + 1], (share, head_dim))
            high = log.astype(jnp.bfloat16).astype(jnp.float32)
            mid = (log - high).astype(jnp.bfloat16).astype(jnp.float32)
            low = log - high - mid
            parts = jnp.where(place == 0, high, jnp.where(place == 1, mid, low))
            parts = jnp.where(place < 3, parts, 0.0).astype(jnp.bfloat16)
            state = states[h].astype(jnp.bfloat16)
            for n in range(shares):
                to = h * shares + n
                packed_ref[to, tokens : tokens + share, :] = state[n * share : (n + 1) * share]
                packed_ref[to, tokens + share :, :] = parts

    return pl.pallas_call(
        kernel,
        in_specs=[WHOLE] * 6,
        out_specs=[VMEM] * 5,
        out_shape=[
            jax.ShapeDtypeStruct((soft_heads, tokens + 2 * share, width), jnp.bfloat16),
            jax.ShapeDtypeStruct(keys.shape, jnp.float32),
            jax.ShapeDtypeStruct(keys.shape, jnp.bfloat16),
            jax.ShapeDtypeStruct((blocks, heads, head_dim, head_dim), jnp.float32),
            jax.ShapeDtypeStruct((blocks * heads, head_dim), jnp.float32),
        ],
        cost_estimate=pl.CostEstimate(
            flops=4 * 10**9, bytes_accessed=6 * 2**20, transcendentals=2**20
        ),
        compiler_params=limits(60),
    )(codes, exponents, query, keys, values, decay_rows)


def entering_states(arrived, tokens):
    seq_count, rows, head_dim = arrived.shape
    share = (rows - tokens) // 2

    def kernel(in_ref, out_ref):
        state = jnp.zeros((share, head_dim), jnp.float32)
        for s in range(seq_count):
            out_ref[s] = state.astype(jnp.bfloat16)
            parts = in_ref[s, tokens + share :, :].astype(jnp.float32)
            fade = jnp.exp(jnp.sum(parts, axis=0, keepdims=True))
            state = fade * state + in_ref[s, tokens : tokens + share, :].astype(jnp.float32)

    return pl.pallas_call(
        kernel,
        in_specs=[VMEM],
        out_specs=VMEM,
        out_shape=jax.ShapeDtypeStruct((seq_count, share, head_dim), jnp.bfloat16),
        compiler_params=limits(8),
    )(arrived)


def finish(returned, tokens, inner, decayed, before, fades):
    soft_heads, rows, width = returned.shape
    blocks, heads, head_dim, _ = before.shape
    shares = soft_heads // heads
    share = rows - tokens

    def kernel(in_ref, inner_ref, decayed_ref, before_ref, fade_ref, soft_ref, lin_ref):
        for h in range(soft_heads):
            soft_ref[:, h * width : (h + 1) * width] = in_ref[h, :tokens, :]
        for h in range(heads):
            cols = slice(h * head_dim, (h + 1) * head_dim)
            entering = in_ref[h * shares : (h + 1) * shares, tokens:, :].astype(jnp.float32)
            entering = entering.reshape(head_dim, head_dim)
            for n in range(blocks):
                span = slice(n * STRETCH, (n + 1) * STRETCH)
                fade = fade_ref[n * heads + h : n * heads + h + 1, :]
                state = (fade * entering + before_ref[n, h]).astype(jnp.bfloat16)
                mixed = inner_ref[span, cols] + jnp.dot(
                    decayed_ref[span, cols], state, preferred_element_type=jnp.float32
                )
                mean = jnp.mean(mixed * mixed, axis=1, keepdims=True)
                lin_ref[span, cols] = (mixed / jnp.sqrt(mean + 1e-06)).astype(jnp.bfloat16)

    return pl.pallas_call(
        kernel,
        in_specs=[VMEM] * 5,
        out_specs=[VMEM] * 2,
        out_shape=[
            jax.ShapeDtypeStruct((tokens, soft_heads * width), jnp.bfloat16),
            jax.ShapeDtypeStruct(inner.shape, jnp.bfloat16),
        ],
        compiler_params=limits(16),
    )(returned, inner, decayed, before, fades)


def shards(
    q_codes, q_exps, k_codes, k_exps, v_codes, v_exps, lin_query, lin_keys, lin_values, decay_log
):
    rank = lax.axis_index("head")
    count = lax.axis_size("head")
    seq_count = lax.axis_size("seq")
    tokens = q_codes.shape[0]
    span = tokens * count

    def ranks(*steps):
        chip, core = rank // 2, rank % 2
        listed = [rank]
        for chips, cores in steps:
            listed.append((chip + chips) % (count // 2) * 2 + (core + cores) % 2)
        return jnp.stack(listed).astype(jnp.int32)

    def exchange(value):
        return lax.all_to_all(value, "seq", split_axis=0, concat_axis=0, tiled=True)

    packed = prepare((k_codes, v_codes), (k_exps.T, v_exps.T))
    own = exchange(packed)
    lin = after((lin_query, lin_keys, lin_values, decay_log.T), packed)
    packed, inner, decayed, before, fades = prepare_rest(q_codes, q_exps.T, *lin, seq_count)
    arrived = exchange(packed)
    own = after(own, packed)
    below = ring(own, 2)
    above = ring(own, -2)
    partner = core_swap(own)
    arrived = after(arrived, below, above)
    outward = jnp.where(rank % 2 == 0, below, above)
    far = lax.ppermute(
        outward, "head", [(i, (i + 2 - i % 2 * 4) % count) for i in range(count)]
    )
    below_other = core_swap(below)
    above_other = core_swap(above)
    state = attend(ranks((0, 0), (0, 1)), arrived, [own, partner], None, span)
    entering = entering_states(arrived, tokens)
    far_other = core_swap(after(far, state[0]))
    state = attend(
        ranks((-1, 0), (-1, 1), (1, 0), (1, 1)),
        arrived,
        [below, below_other, above, above_other],
        state,
        span,
    )
    attended = attend(
        ranks((2, 0), (2, 1)), arrived, [far, far_other], state, span, tail=entering
    )
    returned = exchange(attended)
    return tuple(finish(returned, tokens, inner, decayed, before, fades))


def solution(mesh):
    rows = P(("seq", "head"), None)
    tiles = P("seq", "head")
    return jax.shard_map(
        shards,
        mesh=mesh,
        in_specs=(rows,) * 6 + (tiles,) * 4,
        out_specs=(rows, tiles),
        check_vma=False,
    )
```

```python
import math

import jax
import jax.numpy as jnp
from jax import lax
from jax.experimental import pallas as pl
from jax.experimental.pallas import tpu as pltpu
from jax.sharding import PartitionSpec as P

STRETCH = 128
TILE = 512
KEYS = 256
HIDDEN = -1e30
VMEM = pl.BlockSpec(memory_space=pltpu.VMEM)
SMEM = pl.BlockSpec(memory_space=pltpu.SMEM)
ANY = pl.BlockSpec(memory_space=pl.ANY)
WHOLE = pl.BlockSpec()


def limits(megabytes):
    return pltpu.CompilerParams(vmem_limit_bytes=megabytes * 1024 * 1024)


def core_swap(value):
    count = lax.axis_size("head")
    return lax.ppermute(value, "head", [(i, i ^ 1) for i in range(count)])


def after(value, *others):
    return lax.optimization_barrier((value, *others))[0]


def prepare(codes, exponents):
    heads, tokens = exponents[0].shape
    width = codes[0].shape[1] // heads
    count = len(codes)

    def kernel(*refs):
        out = refs[-1]
        row = lax.broadcasted_iota(jnp.int32, (heads, width), 0)
        for n in range(count):
            scale = jnp.exp2(refs[count + n][...].astype(jnp.float32)).T.astype(jnp.bfloat16)
            for h in range(heads):
                pick = jnp.where(row == h, 1.0, 0.0).astype(jnp.bfloat16)
                wide = jnp.dot(scale, pick, preferred_element_type=jnp.float32)
                rows = refs[n][:, h * width : (h + 1) * width].astype(jnp.float32) * wide
                out[h, n * tokens : (n + 1) * tokens, :] = rows.astype(jnp.bfloat16)

    return pl.pallas_call(
        kernel,
        in_specs=[WHOLE] * (2 * count),
        out_specs=VMEM,
        out_shape=jax.ShapeDtypeStruct((heads, count * tokens, width), jnp.bfloat16),
        compiler_params=limits(60),
    )(*codes, *exponents)


def attend(ranks, query, chunks, state, span, tail=None):
    seq_count, key_dev, head_dim = chunks[0].shape
    key_dev //= 2
    finish = tail is not None
    rows = seq_count * key_dev
    per = TILE // key_dev
    tiles = rows // TILE
    order = [*range(0, tiles, 2), *range(tiles - 1, 0, -2)]
    early = (order[0] + 1) * per
    chunk_count = len(chunks)
    pairs = chunk_count // 2
    scale = math.log2(math.e) / math.sqrt(head_dim)
    first = state is None

    def kernel(*refs):
        refs = list(refs)
        ranks_ref, q_ref = refs.pop(0), refs.pop(0)
        sources = [refs.pop(0) for _ in chunks]
        given = [] if first else [refs.pop(0) for _ in range(3)]
        tail_ref = refs.pop(0) if finish else None
        o_ref = refs.pop(0) if finish else None
        m_ref, l_ref, acc_ref, held, sems, score_a, score_b = refs
        score_refs = (score_a, score_b)
        parts = (slice(0, early), slice(early, seq_count))
        copies = [
            [
                pltpu.make_async_copy(sources[n].at[part], held.at[n, part], sems.at[n, m])
                for n in range(chunk_count)
            ]
            for m, part in enumerate(parts)
        ]
        for copy in copies[0] + copies[1]:
            copy.start()
        if finish:
            o_ref[:, key_dev:, :] = tail_ref[...]
        if first:
            m_ref[...] = jnp.full_like(m_ref, HIDDEN)
            l_ref[...] = jnp.zeros_like(l_ref)
            acc_ref[...] = jnp.zeros_like(acc_ref)
        else:
            m_ref[...] = given[0][...]
            l_ref[...] = given[1][...]
            acc_ref[...] = given[2][...]
        own = ranks_ref[0]

        def units(i):
            return [(c, j) for c in range(2) for j in range((i + 1) * TILE // KEYS)]

        def first_column(i, j):
            return max(0, j * KEYS - i * TILE)

        def joined(old, new, start, how):
            if old is None:
                return new
            if start == 0:
                return how(old, new)
            return jnp.concatenate([old[:, :start], how(old[:, start:], new)], axis=1)

        def produce(p, slot, i, n, q, top):
            c, j = units(i)[n]
            start = first_column(i, j)
            blocks = slice(j * KEYS // key_dev, (j + 1) * KEYS // key_dev)
            keys = held[2 * p + c, blocks, :key_dev, :].reshape(KEYS, head_dim)
            s = lax.dot_general(
                keys, q[start:], (((1,), (1,)), ((), ())), preferred_element_type=jnp.float32
            )
            if j * KEYS >= i * TILE:
                a = lax.broadcasted_iota(jnp.int32, (KEYS, KEYS), 0)
                b = lax.broadcasted_iota(jnp.int32, (KEYS, KEYS), 1)
                key_pos = a // key_dev * span + ranks_ref[1 + 2 * p + c] * key_dev + a % key_dev
                query_pos = b // key_dev * span + own * key_dev + b % key_dev
                corner = jnp.where(key_pos <= query_pos, s[:, :KEYS], HIDDEN)
                if s.shape[1] > KEYS:
                    corner = jnp.concatenate([corner, s[:, KEYS:]], axis=1)
                s = corner
            score_refs[slot][n * KEYS : (n + 1) * KEYS, start:] = s
            part = jnp.max(s.reshape(KEYS // 8, 8, TILE - start), axis=0)
            return joined(top, part, start, jnp.maximum)

        def consume(p, slot, i, n, offset, total, weighted):
            c, j = units(i)[n]
            start = first_column(i, j)
            s = score_refs[slot][n * KEYS : (n + 1) * KEYS, start:]
            w = jnp.exp2(s * scale - offset[:, start:])
            blocks = slice(j * KEYS // key_dev, (j + 1) * KEYS // key_dev)
            values = held[2 * p + c, blocks, key_dev:, :].reshape(KEYS, head_dim)
            x = lax.dot_general(
                values,
                w.astype(jnp.bfloat16),
                (((0,), (0,)), ((), ())),
                preferred_element_type=jnp.float32,
            )
            part = jnp.sum(w.reshape(KEYS // 8, 8, TILE - start), axis=0)
            return joined(total, part, start, jnp.add), joined(weighted, x, start, jnp.add)

        def stage(p, at, before):
            i = order[at % tiles] if at < tiles or pairs > 1 else None
            source = p if at < tiles else jnp.minimum(p + 1, pairs - 1)
            done = order[at - 1] if at > 0 else None
            here, there = at % 2, (at + 1) % 2
            ahead = behind = 0
            if i is not None:
                q = q_ref[i * per : (i + 1) * per, :key_dev, :].reshape(TILE, head_dim)
                ahead = len(units(i))
            if done is not None:
                cols = slice(done * TILE, (done + 1) * TILE)
                old = m_ref[done : done + 1, :]
                new = jnp.maximum(old, jnp.max(before, axis=0, keepdims=True))
                m_ref[done : done + 1, :] = new
                fade = jnp.exp2((old - new) * scale)
                offset = new * scale
                behind = len(units(done))
            top = total = weighted = None
            a = b = 0
            while a < ahead or b < behind:
                if a < ahead and (b >= behind or a * behind <= b * ahead):
                    top = produce(source, here, i, a, q, top)
                    a += 1
                else:
                    total, weighted = consume(p, there, done, b, offset, total, weighted)
                    b += 1
            if done is not None:
                total = l_ref[done : done + 1, :] * fade + jnp.sum(total, axis=0, keepdims=True)
                weighted = acc_ref[:, cols] * fade + weighted
                if finish:
                    o = (weighted / total).T.astype(jnp.bfloat16).reshape(per, key_dev, head_dim)
                    o_ref[done * per : (done + 1) * per, :key_dev, :] = o
                else:
                    l_ref[done : done + 1, :] = total
                    acc_ref[:, cols] = weighted

            @pl.when(own < 0)
            def _():
                m_ref[0:1, :] = jnp.zeros((1, TILE), jnp.float32)

            return top

        def arrive(p, m):
            for n in range(chunk_count):

                @pl.when(p == n // 2)
                def _(n=n):
                    copies[m][n].wait()

        def step(p, top):
            for at in range(1, tiles + 1):
                if at == 1:
                    arrive(p, 1)
                if at == tiles:
                    arrive(p + 1, 0)
                top = stage(p, at, top)
            return top

        arrive(0, 0)
        top = stage(0, 0, None)
        if pairs > 1:
            lax.fori_loop(0, pairs, step, top)
        else:
            step(0, top)

    state_shape = [
        jax.ShapeDtypeStruct((tiles, TILE), jnp.float32),
        jax.ShapeDtypeStruct((tiles, TILE), jnp.float32),
        jax.ShapeDtypeStruct((head_dim, rows), jnp.float32),
    ]
    scratch = [
        pltpu.VMEM((chunk_count, seq_count, 2 * key_dev, head_dim), jnp.bfloat16),
        pltpu.SemaphoreType.DMA((chunk_count, 2)),
        pltpu.VMEM((2 * rows, TILE), jnp.float32),
        pltpu.VMEM((2 * rows, TILE), jnp.float32),
    ]
    if finish:
        out_rows = key_dev + tail.shape[1]
        out_shape = jax.ShapeDtypeStruct((seq_count, out_rows, head_dim), jnp.bfloat16)
        out_specs = VMEM
        scratch = [pltpu.VMEM(s.shape, s.dtype) for s in state_shape] + scratch
    else:
        out_shape, out_specs = state_shape, [VMEM] * 3
    extra = ([] if first else [*state]) + ([tail] if finish else [])
    return pl.pallas_call(
        kernel,
        in_specs=[SMEM, VMEM] + [ANY] * chunk_count + [VMEM] * len(extra),
        out_specs=out_specs,
        out_shape=out_shape,
        scratch_shapes=scratch,
        compiler_params=limits(36),
    )(ranks, query, *chunks, *extra)


def summed(decay):
    tokens = decay.shape[1]
    a = lax.broadcasted_iota(jnp.int32, (tokens, tokens), 0)
    b = lax.broadcasted_iota(jnp.int32, (tokens, tokens), 1)
    ones = jnp.where(a <= b, 1.0, 0.0).astype(jnp.float32)
    cum = jnp.dot(
        decay, ones, precision=lax.Precision.HIGHEST, preferred_element_type=jnp.float32
    )
    return cum, cum.T


def prepare_rest(codes, exponents, query, keys, values, decay_rows, seq_count):
    soft_heads, tokens = exponents.shape
    width = codes.shape[1] // soft_heads
    rows = keys.shape[0]
    heads = decay_rows.shape[0]
    head_dim = keys.shape[1] // heads
    blocks = rows // STRETCH
    shares = seq_count // heads
    share = head_dim // shares

    def kernel(code_ref, exps_ref, q_ref, k_ref, v_ref, decay_ref, *out):
        packed_ref, inner_ref, decayed_ref, before_ref, fade_ref = out
        scale = jnp.exp2(exps_ref[...].astype(jnp.float32)).T
        for h in range(soft_heads):
            part = code_ref[:, h * width : (h + 1) * width].astype(jnp.float32)
            packed_ref[h, :tokens, :] = (part * scale[:, h : h + 1]).astype(jnp.bfloat16)
        a = lax.broadcasted_iota(jnp.int32, (STRETCH, STRETCH), 0)
        b = lax.broadcasted_iota(jnp.int32, (STRETCH, STRETCH), 1)
        causal = b <= a
        place = lax.broadcasted_iota(jnp.int32, (share, head_dim), 0)
        states = [jnp.zeros((head_dim, head_dim), jnp.float32)] * heads
        log_total = jnp.zeros((heads, 1), jnp.float32)
        for n in range(blocks):
            span = slice(n * STRETCH, (n + 1) * STRETCH)
            cum, cum_cols = summed(decay_ref[:, span])
            for h in range(heads):
                cols = slice(h * head_dim, (h + 1) * head_dim)
                q, k, v = q_ref[span, cols], k_ref[span, cols], v_ref[span, cols]
                here, end = cum_cols[:, h : h + 1], cum[h : h + 1, STRETCH - 1 : STRETCH]
                scores = lax.dot_general(
                    q, k, (((1,), (1,)), ((), ())), preferred_element_type=jnp.float32
                )
                gap = jnp.where(causal, here - cum[h : h + 1], 0.0)
                weights = jnp.where(causal, scores * jnp.exp(gap), 0.0).astype(jnp.bfloat16)
                inner_ref[span, cols] = jnp.dot(weights, v, preferred_element_type=jnp.float32)
                decayed = (q.astype(jnp.float32) * jnp.exp(here)).astype(jnp.bfloat16)
                decayed_ref[span, cols] = decayed
                before_ref[n, h] = states[h]
                fade = jnp.exp(log_total[h : h + 1])
                fade_ref[n * heads + h : n * heads + h + 1, :] = jnp.broadcast_to(
                    fade, (1, head_dim)
                )
                aged = (k.astype(jnp.float32) * jnp.exp(end - here)).astype(jnp.bfloat16)
                states[h] = jnp.exp(end) * states[h] + lax.dot_general(
                    aged, v, (((0,), (0,)), ((), ())), preferred_element_type=jnp.float32
                )
            log_total += cum[:, STRETCH - 1 : STRETCH]
        for h in range(heads):
            log = jnp.broadcast_to(log_total[h : h + 1], (share, head_dim))
            high = log.astype(jnp.bfloat16).astype(jnp.float32)
            mid = (log - high).astype(jnp.bfloat16).astype(jnp.float32)
            low = log - high - mid
            parts = jnp.where(place == 0, high, jnp.where(place == 1, mid, low))
            parts = jnp.where(place < 3, parts, 0.0).astype(jnp.bfloat16)
            state = states[h].astype(jnp.bfloat16)
            for n in range(shares):
                to = h * shares + n
                packed_ref[to, tokens : tokens + share, :] = state[n * share : (n + 1) * share]
                packed_ref[to, tokens + share :, :] = parts

    return pl.pallas_call(
        kernel,
        in_specs=[WHOLE] * 6,
        out_specs=[VMEM] * 5,
        out_shape=[
            jax.ShapeDtypeStruct((soft_heads, tokens + 2 * share, width), jnp.bfloat16),
            jax.ShapeDtypeStruct(keys.shape, jnp.float32),
            jax.ShapeDtypeStruct(keys.shape, jnp.bfloat16),
            jax.ShapeDtypeStruct((blocks, heads, head_dim, head_dim), jnp.float32),
            jax.ShapeDtypeStruct((blocks * heads, head_dim), jnp.float32),
        ],
        cost_estimate=pl.CostEstimate(
            flops=4 * 10**9, bytes_accessed=6 * 2**20, transcendentals=2**20
        ),
        compiler_params=limits(60),
    )(codes, exponents, query, keys, values, decay_rows)


def entering_states(arrived, tokens):
    seq_count, rows, head_dim = arrived.shape
    share = (rows - tokens) // 2

    def kernel(in_ref, out_ref):
        state = jnp.zeros((share, head_dim), jnp.float32)
        for s in range(seq_count):
            out_ref[s] = state.astype(jnp.bfloat16)
            parts = in_ref[s, tokens + share :, :].astype(jnp.float32)
            fade = jnp.exp(jnp.sum(parts, axis=0, keepdims=True))
            state = fade * state + in_ref[s, tokens : tokens + share, :].astype(jnp.float32)

    return pl.pallas_call(
        kernel,
        in_specs=[VMEM],
        out_specs=VMEM,
        out_shape=jax.ShapeDtypeStruct((seq_count, share, head_dim), jnp.bfloat16),
        compiler_params=limits(8),
    )(arrived)


def finish(returned, tokens, inner, decayed, before, fades):
    soft_heads, rows, width = returned.shape
    blocks, heads, head_dim, _ = before.shape
    shares = soft_heads // heads
    share = rows - tokens

    def kernel(in_ref, inner_ref, decayed_ref, before_ref, fade_ref, soft_ref, lin_ref):
        for h in range(soft_heads):
            soft_ref[:, h * width : (h + 1) * width] = in_ref[h, :tokens, :]
        for h in range(heads):
            cols = slice(h * head_dim, (h + 1) * head_dim)
            entering = in_ref[h * shares : (h + 1) * shares, tokens:, :].astype(jnp.float32)
            entering = entering.reshape(head_dim, head_dim)
            for n in range(blocks):
                span = slice(n * STRETCH, (n + 1) * STRETCH)
                fade = fade_ref[n * heads + h : n * heads + h + 1, :]
                state = (fade * entering + before_ref[n, h]).astype(jnp.bfloat16)
                mixed = inner_ref[span, cols] + jnp.dot(
                    decayed_ref[span, cols], state, preferred_element_type=jnp.float32
                )
                mean = jnp.mean(mixed * mixed, axis=1, keepdims=True)
                lin_ref[span, cols] = (mixed / jnp.sqrt(mean + 1e-06)).astype(jnp.bfloat16)

    return pl.pallas_call(
        kernel,
        in_specs=[VMEM] * 5,
        out_specs=[VMEM] * 2,
        out_shape=[
            jax.ShapeDtypeStruct((tokens, soft_heads * width), jnp.bfloat16),
            jax.ShapeDtypeStruct(inner.shape, jnp.bfloat16),
        ],
        compiler_params=limits(16),
    )(returned, inner, decayed, before, fades)


def shards(
    q_codes, q_exps, k_codes, k_exps, v_codes, v_exps, lin_query, lin_keys, lin_values, decay_log
):
    rank = lax.axis_index("head")
    count = lax.axis_size("head")
    seq_count = lax.axis_size("seq")
    tokens = q_codes.shape[0]
    span = tokens * count

    def place(chips, cores):
        chip, core = rank // 2, rank % 2
        chip = (chip + chips * (1 - 2 * core)) % (count // 2)
        return chip * 2 + (core + cores) % 2

    def ranks(*steps):
        return jnp.stack([rank, *(place(*step) for step in steps)]).astype(jnp.int32)

    def exchange(value):
        return lax.all_to_all(value, "seq", split_axis=0, concat_axis=0, tiled=True)

    packed = prepare((k_codes, v_codes), (k_exps.T, v_exps.T))
    own = exchange(packed)
    lin = after((lin_query, lin_keys, lin_values, decay_log.T), packed)
    packed, inner, decayed, before, fades = prepare_rest(q_codes, q_exps.T, *lin, seq_count)
    arrived = exchange(packed)
    own = after(own, packed)
    onward = [(i + 2 - i % 2 * 4) % count for i in range(count)]
    first = lax.ppermute(own, "head", list(enumerate(onward)))
    second = lax.ppermute(own, "head", [(to, i) for i, to in enumerate(onward)])
    partner = core_swap(own)
    far = lax.ppermute(first, "head", list(enumerate(onward)))
    far_other = lax.ppermute(first, "head", [(i, to ^ 1) for i, to in enumerate(onward)])
    arrived = after(arrived, first, second)
    first_other = core_swap(first)
    second_other = core_swap(second)
    state = attend(
        ranks((0, 0), (0, 1), (-1, 0), (1, 1), (1, 0), (-1, 1)),
        arrived,
        [own, partner, first, first_other, second, second_other],
        None,
        span,
    )
    entering = entering_states(arrived, tokens)
    attended = attend(
        ranks((2, 0), (2, 1)), arrived, [far, far_other], state, span, tail=entering
    )
    returned = exchange(attended)
    return tuple(finish(returned, tokens, inner, decayed, before, fades))


def solution(mesh):
    rows = P(("seq", "head"), None)
    tiles = P("seq", "head")
    return jax.shard_map(
        shards,
        mesh=mesh,
        in_specs=(rows,) * 6 + (tiles,) * 4,
        out_specs=(rows, tiles),
        check_vma=False,
    )
```

```python
import math

import jax
import jax.numpy as jnp
from jax import lax
from jax.experimental import pallas as pl
from jax.experimental.pallas import tpu as pltpu
from jax.sharding import PartitionSpec as P

STRETCH = 128
TILE = 512
KEYS = 256
HIDDEN = -1e30
VMEM = pl.BlockSpec(memory_space=pltpu.VMEM)
SMEM = pl.BlockSpec(memory_space=pltpu.SMEM)
ANY = pl.BlockSpec(memory_space=pl.ANY)
WHOLE = pl.BlockSpec()


def limits(megabytes):
    return pltpu.CompilerParams(vmem_limit_bytes=megabytes * 1024 * 1024)


def core_swap(value):
    count = lax.axis_size("head")
    return lax.ppermute(value, "head", [(i, i ^ 1) for i in range(count)])


def after(value, *others):
    return lax.optimization_barrier((value, *others))[0]


def prepare(codes, exponents):
    heads, tokens = exponents[0].shape
    width = codes[0].shape[1] // heads
    count = len(codes)

    def kernel(*refs):
        out = refs[-1]
        row = lax.broadcasted_iota(jnp.int32, (heads, width), 0)
        for n in range(count):
            scale = jnp.exp2(refs[count + n][...].astype(jnp.float32)).T.astype(jnp.bfloat16)
            for h in range(heads):
                pick = jnp.where(row == h, 1.0, 0.0).astype(jnp.bfloat16)
                wide = jnp.dot(scale, pick, preferred_element_type=jnp.float32)
                rows = refs[n][:, h * width : (h + 1) * width].astype(jnp.float32) * wide
                out[h, n * tokens : (n + 1) * tokens, :] = rows.astype(jnp.bfloat16)

    return pl.pallas_call(
        kernel,
        in_specs=[WHOLE] * (2 * count),
        out_specs=VMEM,
        out_shape=jax.ShapeDtypeStruct((heads, count * tokens, width), jnp.bfloat16),
        compiler_params=limits(60),
    )(*codes, *exponents)


def attend(ranks, query, chunks, state, span, tail=None):
    seq_count, key_dev, head_dim = chunks[0].shape
    key_dev //= 2
    finish = tail is not None
    rows = seq_count * key_dev
    per = TILE // key_dev
    tiles = rows // TILE
    order = [*range(0, tiles, 2), *range(tiles - 1, 0, -2)]
    chunk_count = len(chunks)
    pairs = chunk_count // 2
    scale = math.log2(math.e) / math.sqrt(head_dim)
    first = state is None

    def kernel(*refs):
        refs = list(refs)
        ranks_ref, q_ref = refs.pop(0), refs.pop(0)
        sources = [refs.pop(0) for _ in chunks]
        given = [] if first else [refs.pop(0) for _ in range(3)]
        tail_ref = refs.pop(0) if finish else None
        o_ref = refs.pop(0) if finish else None
        m_ref, l_ref, acc_ref, held, sems, score_a, score_b = refs
        score_refs = (score_a, score_b)
        ends = [0, *(min(seq_count, (max(order[: m + 1]) + 1) * per) for m in range(3))]
        parts = [slice(ends[m], ends[m + 1]) for m in range(3)]
        copies = [
            [
                pltpu.make_async_copy(sources[n].at[part], held.at[n, part], sems.at[n, m])
                for n in range(chunk_count)
            ]
            for m, part in enumerate(parts)
        ]
        for copy in copies[0] + copies[1] + copies[2]:
            copy.start()
        if finish:
            o_ref[:, key_dev:, :] = tail_ref[...]
        if first:
            m_ref[...] = jnp.full_like(m_ref, HIDDEN)
            l_ref[...] = jnp.zeros_like(l_ref)
            acc_ref[...] = jnp.zeros_like(acc_ref)
        else:
            m_ref[...] = given[0][...]
            l_ref[...] = given[1][...]
            acc_ref[...] = given[2][...]
        own = ranks_ref[0]

        def units(i):
            return [(c, j) for c in range(2) for j in range((i + 1) * TILE // KEYS)]

        def first_column(i, j):
            return max(0, j * KEYS - i * TILE)

        def joined(old, new, start, how):
            if old is None:
                return new
            if start == 0:
                return how(old, new)
            return jnp.concatenate([old[:, :start], how(old[:, start:], new)], axis=1)

        def produce(p, slot, i, n, q, top):
            c, j = units(i)[n]
            start = first_column(i, j)
            blocks = slice(j * KEYS // key_dev, (j + 1) * KEYS // key_dev)
            keys = held[2 * p + c, blocks, :key_dev, :].reshape(KEYS, head_dim)
            s = lax.dot_general(
                keys, q[start:], (((1,), (1,)), ((), ())), preferred_element_type=jnp.float32
            )
            if j * KEYS >= i * TILE:
                a = lax.broadcasted_iota(jnp.int32, (KEYS, KEYS), 0)
                b = lax.broadcasted_iota(jnp.int32, (KEYS, KEYS), 1)
                key_pos = a // key_dev * span + ranks_ref[1 + 2 * p + c] * key_dev + a % key_dev
                query_pos = b // key_dev * span + own * key_dev + b % key_dev
                corner = jnp.where(key_pos <= query_pos, s[:, :KEYS], HIDDEN)
                if s.shape[1] > KEYS:
                    corner = jnp.concatenate([corner, s[:, KEYS:]], axis=1)
                s = corner
            score_refs[slot][n * KEYS : (n + 1) * KEYS, start:] = s
            part = jnp.max(s.reshape(KEYS // 8, 8, TILE - start), axis=0)
            return joined(top, part, start, jnp.maximum)

        def consume(p, slot, i, n, offset, total, weighted):
            c, j = units(i)[n]
            start = first_column(i, j)
            s = score_refs[slot][n * KEYS : (n + 1) * KEYS, start:]
            w = jnp.exp2(s * scale - offset[:, start:])
            blocks = slice(j * KEYS // key_dev, (j + 1) * KEYS // key_dev)
            values = held[2 * p + c, blocks, key_dev:, :].reshape(KEYS, head_dim)
            x = lax.dot_general(
                values,
                w.astype(jnp.bfloat16),
                (((0,), (0,)), ((), ())),
                preferred_element_type=jnp.float32,
            )
            part = jnp.sum(w.reshape(KEYS // 8, 8, TILE - start), axis=0)
            return joined(total, part, start, jnp.add), joined(weighted, x, start, jnp.add)

        def stage(p, at, before):
            i = order[at % tiles] if at < tiles or pairs > 1 else None
            source = p if at < tiles else jnp.minimum(p + 1, pairs - 1)
            done = order[at - 1] if at > 0 else None
            here, there = at % 2, (at + 1) % 2
            ahead = behind = 0
            if i is not None:
                q = q_ref[i * per : (i + 1) * per, :key_dev, :].reshape(TILE, head_dim)
                ahead = len(units(i))
            if done is not None:
                cols = slice(done * TILE, (done + 1) * TILE)
                old = m_ref[done : done + 1, :]
                new = jnp.maximum(old, jnp.max(before, axis=0, keepdims=True))
                m_ref[done : done + 1, :] = new
                fade = jnp.exp2((old - new) * scale)
                offset = new * scale
                behind = len(units(done))
            top = total = weighted = None
            a = b = 0
            while a < ahead or b < behind:
                if a < ahead and (b >= behind or a * behind <= b * ahead):
                    top = produce(source, here, i, a, q, top)
                    a += 1
                else:
                    total, weighted = consume(p, there, done, b, offset, total, weighted)
                    b += 1
            if done is not None:
                total = l_ref[done : done + 1, :] * fade + jnp.sum(total, axis=0, keepdims=True)
                weighted = acc_ref[:, cols] * fade + weighted
                if finish:
                    o = (weighted / total).T.astype(jnp.bfloat16).reshape(per, key_dev, head_dim)
                    o_ref[done * per : (done + 1) * per, :key_dev, :] = o
                else:
                    l_ref[done : done + 1, :] = total
                    acc_ref[:, cols] = weighted

            @pl.when(own < 0)
            def _():
                m_ref[0:1, :] = jnp.zeros((1, TILE), jnp.float32)

            return top

        def arrive(p, m):
            for n in range(chunk_count):

                @pl.when(p == n // 2)
                def _(n=n):
                    copies[m][n].wait()

        def step(p, top):
            for at in range(1, tiles + 1):
                if at in (1, 2):
                    arrive(p, at)
                if at == tiles:
                    arrive(p + 1, 0)
                top = stage(p, at, top)
            return top

        arrive(0, 0)
        top = stage(0, 0, None)
        if pairs > 1:
            lax.fori_loop(0, pairs, step, top)
        else:
            step(0, top)

    state_shape = [
        jax.ShapeDtypeStruct((tiles, TILE), jnp.float32),
        jax.ShapeDtypeStruct((tiles, TILE), jnp.float32),
        jax.ShapeDtypeStruct((head_dim, rows), jnp.float32),
    ]
    scratch = [
        pltpu.VMEM((chunk_count, seq_count, 2 * key_dev, head_dim), jnp.bfloat16),
        pltpu.SemaphoreType.DMA((chunk_count, 3)),
        pltpu.VMEM((2 * (max(order[0::2]) + 1) * TILE, TILE), jnp.float32),
        pltpu.VMEM((2 * (max(order[1::2]) + 1) * TILE, TILE), jnp.float32),
    ]
    if finish:
        out_rows = key_dev + tail.shape[1]
        out_shape = jax.ShapeDtypeStruct((seq_count, out_rows, head_dim), jnp.bfloat16)
        out_specs = VMEM
        scratch = [pltpu.VMEM(s.shape, s.dtype) for s in state_shape] + scratch
    else:
        out_shape, out_specs = state_shape, [VMEM] * 3
    extra = ([] if first else [*state]) + ([tail] if finish else [])
    return pl.pallas_call(
        kernel,
        in_specs=[SMEM, VMEM] + [ANY] * chunk_count + [VMEM] * len(extra),
        out_specs=out_specs,
        out_shape=out_shape,
        scratch_shapes=scratch,
        compiler_params=limits(25),
    )(ranks, query, *chunks, *extra)


def summed(decay):
    tokens = decay.shape[1]
    a = lax.broadcasted_iota(jnp.int32, (tokens, tokens), 0)
    b = lax.broadcasted_iota(jnp.int32, (tokens, tokens), 1)
    ones = jnp.where(a <= b, 1.0, 0.0).astype(jnp.float32)
    cum = jnp.dot(
        decay, ones, precision=lax.Precision.HIGHEST, preferred_element_type=jnp.float32
    )
    return cum, cum.T


def prepare_rest(codes, exponents, query, keys, values, decay_rows, seq_count):
    soft_heads, tokens = exponents.shape
    width = codes.shape[1] // soft_heads
    rows = keys.shape[0]
    heads = decay_rows.shape[0]
    head_dim = keys.shape[1] // heads
    blocks = rows // STRETCH
    shares = seq_count // heads
    share = head_dim // shares

    def kernel(code_ref, exps_ref, q_ref, k_ref, v_ref, decay_ref, *out):
        packed_ref, inner_ref, decayed_ref, before_ref, fade_ref = out
        scale = jnp.exp2(exps_ref[...].astype(jnp.float32)).T
        for h in range(soft_heads):
            part = code_ref[:, h * width : (h + 1) * width].astype(jnp.float32)
            packed_ref[h, :tokens, :] = (part * scale[:, h : h + 1]).astype(jnp.bfloat16)
        a = lax.broadcasted_iota(jnp.int32, (STRETCH, STRETCH), 0)
        b = lax.broadcasted_iota(jnp.int32, (STRETCH, STRETCH), 1)
        causal = b <= a
        place = lax.broadcasted_iota(jnp.int32, (share, head_dim), 0)
        states = [jnp.zeros((head_dim, head_dim), jnp.float32)] * heads
        log_total = jnp.zeros((heads, 1), jnp.float32)
        for n in range(blocks):
            span = slice(n * STRETCH, (n + 1) * STRETCH)
            cum, cum_cols = summed(decay_ref[:, span])
            for h in range(heads):
                cols = slice(h * head_dim, (h + 1) * head_dim)
                q, k, v = q_ref[span, cols], k_ref[span, cols], v_ref[span, cols]
                here, end = cum_cols[:, h : h + 1], cum[h : h + 1, STRETCH - 1 : STRETCH]
                scores = lax.dot_general(
                    q, k, (((1,), (1,)), ((), ())), preferred_element_type=jnp.float32
                )
                gap = jnp.where(causal, here - cum[h : h + 1], 0.0)
                weights = jnp.where(causal, scores * jnp.exp(gap), 0.0).astype(jnp.bfloat16)
                inner_ref[span, cols] = jnp.dot(weights, v, preferred_element_type=jnp.float32)
                decayed = (q.astype(jnp.float32) * jnp.exp(here)).astype(jnp.bfloat16)
                decayed_ref[span, cols] = decayed
                before_ref[n, h] = states[h]
                fade = jnp.exp(log_total[h : h + 1])
                fade_ref[n * heads + h : n * heads + h + 1, :] = jnp.broadcast_to(
                    fade, (1, head_dim)
                )
                aged = (k.astype(jnp.float32) * jnp.exp(end - here)).astype(jnp.bfloat16)
                states[h] = jnp.exp(end) * states[h] + lax.dot_general(
                    aged, v, (((0,), (0,)), ((), ())), preferred_element_type=jnp.float32
                )
            log_total += cum[:, STRETCH - 1 : STRETCH]
        for h in range(heads):
            log = jnp.broadcast_to(log_total[h : h + 1], (share, head_dim))
            high = log.astype(jnp.bfloat16).astype(jnp.float32)
            mid = (log - high).astype(jnp.bfloat16).astype(jnp.float32)
            low = log - high - mid
            parts = jnp.where(place == 0, high, jnp.where(place == 1, mid, low))
            parts = jnp.where(place < 3, parts, 0.0).astype(jnp.bfloat16)
            state = states[h].astype(jnp.bfloat16)
            for n in range(shares):
                to = h * shares + n
                packed_ref[to, tokens : tokens + share, :] = state[n * share : (n + 1) * share]
                packed_ref[to, tokens + share :, :] = parts

    return pl.pallas_call(
        kernel,
        in_specs=[WHOLE] * 6,
        out_specs=[VMEM] * 5,
        out_shape=[
            jax.ShapeDtypeStruct((soft_heads, tokens + 2 * share, width), jnp.bfloat16),
            jax.ShapeDtypeStruct(keys.shape, jnp.float32),
            jax.ShapeDtypeStruct(keys.shape, jnp.bfloat16),
            jax.ShapeDtypeStruct((blocks, heads, head_dim, head_dim), jnp.float32),
            jax.ShapeDtypeStruct((blocks * heads, head_dim), jnp.float32),
        ],
        cost_estimate=pl.CostEstimate(
            flops=4 * 10**9, bytes_accessed=6 * 2**20, transcendentals=2**20
        ),
        compiler_params=limits(60),
    )(codes, exponents, query, keys, values, decay_rows)


def entering_states(arrived, tokens):
    seq_count, rows, head_dim = arrived.shape
    share = (rows - tokens) // 2

    def kernel(in_ref, out_ref):
        state = jnp.zeros((share, head_dim), jnp.float32)
        for s in range(seq_count):
            out_ref[s] = state.astype(jnp.bfloat16)
            parts = in_ref[s, tokens + share :, :].astype(jnp.float32)
            fade = jnp.exp(jnp.sum(parts, axis=0, keepdims=True))
            state = fade * state + in_ref[s, tokens : tokens + share, :].astype(jnp.float32)

    return pl.pallas_call(
        kernel,
        in_specs=[VMEM],
        out_specs=VMEM,
        out_shape=jax.ShapeDtypeStruct((seq_count, share, head_dim), jnp.bfloat16),
        compiler_params=limits(8),
    )(arrived)


def finish(returned, tokens, inner, decayed, before, fades):
    soft_heads, rows, width = returned.shape
    blocks, heads, head_dim, _ = before.shape
    shares = soft_heads // heads
    share = rows - tokens

    def kernel(in_ref, inner_ref, decayed_ref, before_ref, fade_ref, *rest):
        soft_out, lin_out, soft_ref, lin_ref, sems = rest
        for h in range(soft_heads):
            soft_ref[:, h * width : (h + 1) * width] = in_ref[h, :tokens, :]
        copies = [pltpu.make_async_copy(soft_ref, soft_out, sems.at[blocks])]
        copies[0].start()
        enterings = []
        for h in range(heads):
            entering = in_ref[h * shares : (h + 1) * shares, tokens:, :].astype(jnp.float32)
            enterings.append(entering.reshape(head_dim, head_dim))
        for n in range(blocks):
            span = slice(n * STRETCH, (n + 1) * STRETCH)
            for h in range(heads):
                cols = slice(h * head_dim, (h + 1) * head_dim)
                fade = fade_ref[n * heads + h : n * heads + h + 1, :]
                state = (fade * enterings[h] + before_ref[n, h]).astype(jnp.bfloat16)
                mixed = inner_ref[span, cols] + jnp.dot(
                    decayed_ref[span, cols], state, preferred_element_type=jnp.float32
                )
                mean = jnp.mean(mixed * mixed, axis=1, keepdims=True)
                lin_ref[span, cols] = (mixed / jnp.sqrt(mean + 1e-06)).astype(jnp.bfloat16)
            copies.append(
                pltpu.make_async_copy(lin_ref.at[span], lin_out.at[span], sems.at[n])
            )
            copies[-1].start()
        for copy in copies:
            copy.wait()

    return pl.pallas_call(
        kernel,
        in_specs=[VMEM] * 5,
        out_specs=[ANY] * 2,
        scratch_shapes=[
            pltpu.VMEM((tokens, soft_heads * width), jnp.bfloat16),
            pltpu.VMEM(inner.shape, jnp.bfloat16),
            pltpu.SemaphoreType.DMA((blocks + 1,)),
        ],
        out_shape=[
            jax.ShapeDtypeStruct((tokens, soft_heads * width), jnp.bfloat16),
            jax.ShapeDtypeStruct(inner.shape, jnp.bfloat16),
        ],
        compiler_params=limits(16),
    )(returned, inner, decayed, before, fades)


def shards(
    q_codes, q_exps, k_codes, k_exps, v_codes, v_exps, lin_query, lin_keys, lin_values, decay_log
):
    rank = lax.axis_index("head")
    count = lax.axis_size("head")
    seq_count = lax.axis_size("seq")
    tokens = q_codes.shape[0]
    span = tokens * count

    def place(chips, cores):
        chip, core = rank // 2, rank % 2
        chip = (chip + chips * (1 - 2 * core)) % (count // 2)
        return chip * 2 + (core + cores) % 2

    def ranks(*steps):
        return jnp.stack([rank, *(place(*step) for step in steps)]).astype(jnp.int32)

    def exchange(value):
        return lax.all_to_all(value, "seq", split_axis=0, concat_axis=0, tiled=True)

    packed = prepare((k_codes, v_codes), (k_exps.T, v_exps.T))
    own = exchange(packed)
    lin = after((lin_query, lin_keys, lin_values, decay_log.T), packed)
    packed, inner, decayed, before, fades = prepare_rest(q_codes, q_exps.T, *lin, seq_count)
    arrived = exchange(packed)
    own = after(own, packed)
    onward = [(i + 2 - i % 2 * 4) % count for i in range(count)]
    first = lax.ppermute(own, "head", list(enumerate(onward)))
    second = lax.ppermute(own, "head", [(to, i) for i, to in enumerate(onward)])
    partner = core_swap(own)
    far = lax.ppermute(first, "head", list(enumerate(onward)))
    far_other = lax.ppermute(first, "head", [(i, to ^ 1) for i, to in enumerate(onward)])
    arrived = after(arrived, first, second)
    first_other = core_swap(first)
    second_other = core_swap(second)
    state = attend(
        ranks((0, 0), (0, 1), (-1, 0), (1, 1), (1, 0), (-1, 1)),
        arrived,
        [own, partner, first, first_other, second, second_other],
        None,
        span,
    )
    entering = entering_states(arrived, tokens)
    attended = attend(
        ranks((2, 0), (2, 1)), arrived, [far, far_other], state, span, tail=entering
    )
    returned = exchange(attended)
    return tuple(finish(returned, tokens, inner, decayed, before, fades))


def solution(mesh):
    rows = P(("seq", "head"), None)
    tiles = P("seq", "head")
    return jax.shard_map(
        shards,
        mesh=mesh,
        in_specs=(rows,) * 6 + (tiles,) * 4,
        out_specs=(rows, tiles),
        check_vma=False,
    )
```

```python
import math

import jax
import jax.numpy as jnp
from jax import lax
from jax.experimental import pallas as pl
from jax.experimental.pallas import tpu as pltpu
from jax.sharding import PartitionSpec as P

STRETCH = 128
TILE = 512
KEYS = 256
HIDDEN = -1e30
VMEM = pl.BlockSpec(memory_space=pltpu.VMEM)
SMEM = pl.BlockSpec(memory_space=pltpu.SMEM)
ANY = pl.BlockSpec(memory_space=pl.ANY)
WHOLE = pl.BlockSpec()


def limits(megabytes):
    return pltpu.CompilerParams(vmem_limit_bytes=megabytes * 1024 * 1024)


def core_swap(value):
    count = lax.axis_size("head")
    return lax.ppermute(value, "head", [(i, i ^ 1) for i in range(count)])


def after(value, *others):
    return lax.optimization_barrier((value, *others))[0]


def prepare(codes, exponents):
    heads, tokens = exponents[0].shape
    width = codes[0].shape[1] // heads
    count = len(codes)

    def kernel(*refs):
        out = refs[-1]
        row = lax.broadcasted_iota(jnp.int32, (heads, width), 0)
        for n in range(count):
            scale = jnp.exp2(refs[count + n][...].astype(jnp.float32)).T.astype(jnp.bfloat16)
            for h in range(heads):
                pick = jnp.where(row == h, 1.0, 0.0).astype(jnp.bfloat16)
                wide = jnp.dot(scale, pick, preferred_element_type=jnp.float32)
                rows = refs[n][:, h * width : (h + 1) * width].astype(jnp.float32) * wide
                out[h, n * tokens : (n + 1) * tokens, :] = rows.astype(jnp.bfloat16)

    return pl.pallas_call(
        kernel,
        in_specs=[WHOLE] * (2 * count),
        out_specs=VMEM,
        out_shape=jax.ShapeDtypeStruct((heads, count * tokens, width), jnp.bfloat16),
        compiler_params=limits(60),
    )(*codes, *exponents)


def attend(ranks, query, chunks, state, span, tail=None):
    seq_count, key_dev, head_dim = chunks[0].shape
    key_dev //= 2
    finish = tail is not None
    rows = seq_count * key_dev
    per = TILE // key_dev
    tiles = rows // TILE
    order = [*range(0, tiles, 2), *range(tiles - 1, 0, -2)]
    chunk_count = len(chunks)
    pairs = chunk_count // 2
    scale = math.log2(math.e) / math.sqrt(head_dim)
    first = state is None

    def kernel(*refs):
        refs = list(refs)
        ranks_ref, q_ref = refs.pop(0), refs.pop(0)
        sources = [refs.pop(0) for _ in chunks]
        given = [] if first else [refs.pop(0) for _ in range(3)]
        tail_ref = refs.pop(0) if finish else None
        o_ref = refs.pop(0) if finish else None
        m_ref, l_ref, acc_ref, held, sems, score_a, score_b = refs
        score_refs = (score_a, score_b)
        ends = [0, *(min(seq_count, (max(order[: m + 1]) + 1) * per) for m in range(3))]
        parts = [slice(ends[m], ends[m + 1]) for m in range(3)]
        copies = [
            [
                pltpu.make_async_copy(sources[n].at[part], held.at[n, part], sems.at[n, m])
                for n in range(chunk_count)
            ]
            for m, part in enumerate(parts)
        ]
        for copy in copies[0] + copies[1] + copies[2]:
            copy.start()
        if finish:
            o_ref[:, key_dev:, :] = tail_ref[...]
        if first:
            m_ref[...] = jnp.full_like(m_ref, HIDDEN)
            l_ref[...] = jnp.zeros_like(l_ref)
            acc_ref[...] = jnp.zeros_like(acc_ref)
        else:
            m_ref[...] = given[0][...]
            l_ref[...] = given[1][...]
            acc_ref[...] = given[2][...]
        own = ranks_ref[0]

        def units(i):
            return [(c, j) for c in range(2) for j in range((i + 1) * TILE // KEYS)]

        def first_column(i, j):
            return max(0, j * KEYS - i * TILE)

        def joined(old, new, start, how):
            if old is None:
                return new
            if start == 0:
                return how(old, new)
            return jnp.concatenate([old[:, :start], how(old[:, start:], new)], axis=1)

        def produce(p, slot, i, n, q, top):
            c, j = units(i)[n]
            start = first_column(i, j)
            blocks = slice(j * KEYS // key_dev, (j + 1) * KEYS // key_dev)
            keys = held[2 * p + c, blocks, :key_dev, :].reshape(KEYS, head_dim)
            s = lax.dot_general(
                keys, q[start:], (((1,), (1,)), ((), ())), preferred_element_type=jnp.float32
            )
            if j * KEYS >= i * TILE:
                a = lax.broadcasted_iota(jnp.int32, (KEYS, KEYS), 0)
                b = lax.broadcasted_iota(jnp.int32, (KEYS, KEYS), 1)
                key_pos = a // key_dev * span + ranks_ref[1 + 2 * p + c] * key_dev + a % key_dev
                query_pos = b // key_dev * span + own * key_dev + b % key_dev
                corner = jnp.where(key_pos <= query_pos, s[:, :KEYS], HIDDEN)
                if s.shape[1] > KEYS:
                    corner = jnp.concatenate([corner, s[:, KEYS:]], axis=1)
                s = corner
            score_refs[slot][n * KEYS : (n + 1) * KEYS, start:] = s
            part = jnp.max(s.reshape(KEYS // 8, 8, TILE - start), axis=0)
            return joined(top, part, start, jnp.maximum)

        def consume(p, slot, i, n, offset, total, weighted):
            c, j = units(i)[n]
            start = first_column(i, j)
            s = score_refs[slot][n * KEYS : (n + 1) * KEYS, start:]
            w = jnp.exp2(s * scale - offset[:, start:])
            blocks = slice(j * KEYS // key_dev, (j + 1) * KEYS // key_dev)
            values = held[2 * p + c, blocks, key_dev:, :].reshape(KEYS, head_dim)
            x = lax.dot_general(
                values,
                w.astype(jnp.bfloat16),
                (((0,), (0,)), ((), ())),
                preferred_element_type=jnp.float32,
            )
            part = jnp.sum(w.reshape(KEYS // 8, 8, TILE - start), axis=0)
            return joined(total, part, start, jnp.add), joined(weighted, x, start, jnp.add)

        def stage(p, at, before):
            i = order[at % tiles] if at < tiles or pairs > 1 else None
            source = p if at < tiles else jnp.minimum(p + 1, pairs - 1)
            done = order[at - 1] if at > 0 else None
            here, there = at % 2, (at + 1) % 2
            ahead = behind = 0
            if i is not None:
                q = q_ref[i * per : (i + 1) * per, :key_dev, :].reshape(TILE, head_dim)
                ahead = len(units(i))
            if done is not None:
                cols = slice(done * TILE, (done + 1) * TILE)
                old = m_ref[done : done + 1, :]
                new = jnp.maximum(old, jnp.max(before, axis=0, keepdims=True))
                m_ref[done : done + 1, :] = new
                fade = jnp.exp2((old - new) * scale)
                offset = new * scale
                behind = len(units(done))
            top = total = weighted = None
            a = b = 0
            while a < ahead or b < behind:
                if a < ahead and (b >= behind or a * behind <= b * ahead):
                    top = produce(source, here, i, a, q, top)
                    a += 1
                else:
                    total, weighted = consume(p, there, done, b, offset, total, weighted)
                    b += 1
            if done is not None:
                total = l_ref[done : done + 1, :] * fade + jnp.sum(total, axis=0, keepdims=True)
                weighted = acc_ref[:, cols] * fade + weighted
                if finish:
                    o = (weighted / total).T.astype(jnp.bfloat16).reshape(per, key_dev, head_dim)
                    o_ref[done * per : (done + 1) * per, :key_dev, :] = o
                else:
                    l_ref[done : done + 1, :] = total
                    acc_ref[:, cols] = weighted

            @pl.when(own < 0)
            def _():
                m_ref[0:1, :] = jnp.zeros((1, TILE), jnp.float32)

            return top

        def arrive(p, m):
            for n in range(chunk_count):

                @pl.when(p == n // 2)
                def _(n=n):
                    copies[m][n].wait()

        def step(p, top):
            for at in range(1, tiles + 1):
                if at in (1, 2):
                    arrive(p, at)
                if at == tiles:
                    arrive(p + 1, 0)
                top = stage(p, at, top)
            return top

        arrive(0, 0)
        top = stage(0, 0, None)
        if pairs > 1:
            lax.fori_loop(0, pairs, step, top)
        else:
            step(0, top)

    state_shape = [
        jax.ShapeDtypeStruct((tiles, TILE), jnp.float32),
        jax.ShapeDtypeStruct((tiles, TILE), jnp.float32),
        jax.ShapeDtypeStruct((head_dim, rows), jnp.float32),
    ]
    scratch = [
        pltpu.VMEM((chunk_count, seq_count, 2 * key_dev, head_dim), jnp.bfloat16),
        pltpu.SemaphoreType.DMA((chunk_count, 3)),
        pltpu.VMEM((2 * (max(order[0::2]) + 1) * TILE, TILE), jnp.float32),
        pltpu.VMEM((2 * (max(order[1::2]) + 1) * TILE, TILE), jnp.float32),
    ]
    if finish:
        out_rows = key_dev + tail.shape[1]
        out_shape = jax.ShapeDtypeStruct((seq_count, out_rows, head_dim), jnp.bfloat16)
        out_specs = VMEM
        scratch = [pltpu.VMEM(s.shape, s.dtype) for s in state_shape] + scratch
    else:
        out_shape, out_specs = state_shape, [VMEM] * 3
    extra = ([] if first else [*state]) + ([tail] if finish else [])
    return pl.pallas_call(
        kernel,
        in_specs=[SMEM, VMEM] + [ANY] * chunk_count + [VMEM] * len(extra),
        out_specs=out_specs,
        out_shape=out_shape,
        scratch_shapes=scratch,
        compiler_params=limits(25),
    )(ranks, query, *chunks, *extra)


def summed(decay):
    tokens = decay.shape[1]
    a = lax.broadcasted_iota(jnp.int32, (tokens, tokens), 0)
    b = lax.broadcasted_iota(jnp.int32, (tokens, tokens), 1)
    ones = jnp.where(a <= b, 1.0, 0.0).astype(jnp.float32)
    cum = jnp.dot(
        decay, ones, precision=lax.Precision.HIGHEST, preferred_element_type=jnp.float32
    )
    return cum, cum.T


def prepare_rest(codes, exponents, query, keys, values, decay_rows, seq_count):
    soft_heads, tokens = exponents.shape
    width = codes.shape[1] // soft_heads
    rows = keys.shape[0]
    heads = decay_rows.shape[0]
    head_dim = keys.shape[1] // heads
    blocks = rows // STRETCH
    shares = seq_count // heads
    share = head_dim // shares

    def kernel(code_ref, exps_ref, q_ref, k_ref, v_ref, decay_ref, *out):
        packed_ref, inner_ref, decayed_ref, before_ref, fade_ref = out
        scale = jnp.exp2(exps_ref[...].astype(jnp.float32)).T
        for h in range(soft_heads):
            part = code_ref[:, h * width : (h + 1) * width].astype(jnp.float32)
            packed_ref[h, :tokens, :] = (part * scale[:, h : h + 1]).astype(jnp.bfloat16)
        a = lax.broadcasted_iota(jnp.int32, (STRETCH, STRETCH), 0)
        b = lax.broadcasted_iota(jnp.int32, (STRETCH, STRETCH), 1)
        causal = b <= a
        place = lax.broadcasted_iota(jnp.int32, (share, head_dim), 0)
        states = [jnp.zeros((head_dim, head_dim), jnp.float32)] * heads
        log_total = jnp.zeros((heads, 1), jnp.float32)
        for n in range(blocks):
            span = slice(n * STRETCH, (n + 1) * STRETCH)
            cum, cum_cols = summed(decay_ref[:, span])
            for h in range(heads):
                cols = slice(h * head_dim, (h + 1) * head_dim)
                q, k, v = q_ref[span, cols], k_ref[span, cols], v_ref[span, cols]
                here, end = cum_cols[:, h : h + 1], cum[h : h + 1, STRETCH - 1 : STRETCH]
                scores = lax.dot_general(
                    q, k, (((1,), (1,)), ((), ())), preferred_element_type=jnp.float32
                )
                gap = jnp.where(causal, here - cum[h : h + 1], 0.0)
                weights = jnp.where(causal, scores * jnp.exp(gap), 0.0).astype(jnp.bfloat16)
                inner_ref[span, cols] = jnp.dot(weights, v, preferred_element_type=jnp.float32)
                decayed = (q.astype(jnp.float32) * jnp.exp(here)).astype(jnp.bfloat16)
                decayed_ref[span, cols] = decayed
                before_ref[n, h] = states[h]
                fade = jnp.exp(log_total[h : h + 1])
                fade_ref[n * heads + h : n * heads + h + 1, :] = jnp.broadcast_to(
                    fade, (1, head_dim)
                )
                aged = (k.astype(jnp.float32) * jnp.exp(end - here)).astype(jnp.bfloat16)
                states[h] = jnp.exp(end) * states[h] + lax.dot_general(
                    aged, v, (((0,), (0,)), ((), ())), preferred_element_type=jnp.float32
                )
            log_total += cum[:, STRETCH - 1 : STRETCH]
        for h in range(heads):
            log = jnp.broadcast_to(log_total[h : h + 1], (share, head_dim))
            high = log.astype(jnp.bfloat16).astype(jnp.float32)
            mid = (log - high).astype(jnp.bfloat16).astype(jnp.float32)
            low = log - high - mid
            parts = jnp.where(place == 0, high, jnp.where(place == 1, mid, low))
            parts = jnp.where(place < 3, parts, 0.0).astype(jnp.bfloat16)
            state = states[h].astype(jnp.bfloat16)
            for n in range(shares):
                to = h * shares + n
                packed_ref[to, tokens : tokens + share, :] = state[n * share : (n + 1) * share]
                packed_ref[to, tokens + share :, :] = parts

    return pl.pallas_call(
        kernel,
        in_specs=[WHOLE] * 6,
        out_specs=[VMEM] * 5,
        out_shape=[
            jax.ShapeDtypeStruct((soft_heads, tokens + 2 * share, width), jnp.bfloat16),
            jax.ShapeDtypeStruct(keys.shape, jnp.float32),
            jax.ShapeDtypeStruct(keys.shape, jnp.bfloat16),
            jax.ShapeDtypeStruct((blocks, heads, head_dim, head_dim), jnp.float32),
            jax.ShapeDtypeStruct((blocks * heads, head_dim), jnp.float32),
        ],
        cost_estimate=pl.CostEstimate(
            flops=4 * 10**9, bytes_accessed=6 * 2**20, transcendentals=2**20
        ),
        compiler_params=limits(60),
    )(codes, exponents, query, keys, values, decay_rows)


def entering_states(arrived, tokens):
    seq_count, rows, head_dim = arrived.shape
    share = (rows - tokens) // 2

    def kernel(in_ref, out_ref):
        state = jnp.zeros((share, head_dim), jnp.float32)
        for s in range(seq_count):
            out_ref[s] = state.astype(jnp.bfloat16)
            parts = in_ref[s, tokens + share :, :].astype(jnp.float32)
            fade = jnp.exp(jnp.sum(parts, axis=0, keepdims=True))
            state = fade * state + in_ref[s, tokens : tokens + share, :].astype(jnp.float32)

    return pl.pallas_call(
        kernel,
        in_specs=[VMEM],
        out_specs=VMEM,
        out_shape=jax.ShapeDtypeStruct((seq_count, share, head_dim), jnp.bfloat16),
        compiler_params=limits(8),
    )(arrived)


def finish(returned, tokens, inner, decayed, before, fades):
    soft_heads, rows, width = returned.shape
    blocks, heads, head_dim, _ = before.shape
    shares = soft_heads // heads
    share = rows - tokens

    def kernel(in_ref, inner_ref, decayed_ref, before_ref, fade_ref, *rest):
        soft_out, lin_out, soft_ref, lin_ref, sems = rest
        for h in range(soft_heads):
            soft_ref[:, h * width : (h + 1) * width] = in_ref[h, :tokens, :]
        copies = [pltpu.make_async_copy(soft_ref, soft_out, sems.at[blocks])]
        copies[0].start()
        enterings = []
        for h in range(heads):
            entering = in_ref[h * shares : (h + 1) * shares, tokens:, :].astype(jnp.float32)
            enterings.append(entering.reshape(head_dim, head_dim))
        for n in range(blocks):
            span = slice(n * STRETCH, (n + 1) * STRETCH)
            for h in range(heads):
                cols = slice(h * head_dim, (h + 1) * head_dim)
                fade = fade_ref[n * heads + h : n * heads + h + 1, :]
                state = (fade * enterings[h] + before_ref[n, h]).astype(jnp.bfloat16)
                mixed = inner_ref[span, cols] + jnp.dot(
                    decayed_ref[span, cols], state, preferred_element_type=jnp.float32
                )
                mean = jnp.mean(mixed * mixed, axis=1, keepdims=True)
                lin_ref[span, cols] = (mixed / jnp.sqrt(mean + 1e-06)).astype(jnp.bfloat16)
            copies.append(
                pltpu.make_async_copy(lin_ref.at[span], lin_out.at[span], sems.at[n])
            )
            copies[-1].start()
        for copy in copies:
            copy.wait()

    return pl.pallas_call(
        kernel,
        in_specs=[VMEM] * 5,
        out_specs=[ANY] * 2,
        scratch_shapes=[
            pltpu.VMEM((tokens, soft_heads * width), jnp.bfloat16),
            pltpu.VMEM(inner.shape, jnp.bfloat16),
            pltpu.SemaphoreType.DMA((blocks + 1,)),
        ],
        out_shape=[
            jax.ShapeDtypeStruct((tokens, soft_heads * width), jnp.bfloat16),
            jax.ShapeDtypeStruct(inner.shape, jnp.bfloat16),
        ],
        compiler_params=limits(16),
    )(returned, inner, decayed, before, fades)


def shards(
    q_codes, q_exps, k_codes, k_exps, v_codes, v_exps, lin_query, lin_keys, lin_values, decay_log
):
    rank = lax.axis_index("head")
    count = lax.axis_size("head")
    seq_count = lax.axis_size("seq")
    tokens = q_codes.shape[0]
    span = tokens * count

    def place(chips, cores):
        chip, core = rank // 2, rank % 2
        chip = (chip + chips * (1 - 2 * core)) % (count // 2)
        return chip * 2 + (core + cores) % 2

    def ranks(*steps):
        return jnp.stack([rank, *(place(*step) for step in steps)]).astype(jnp.int32)

    def exchange(value):
        return lax.all_to_all(value, "seq", split_axis=0, concat_axis=0, tiled=True)

    packed = prepare((k_codes, v_codes), (k_exps.T, v_exps.T))
    own = exchange(packed)
    lin = after((lin_query, lin_keys, lin_values, decay_log.T), packed)
    packed, inner, decayed, before, fades = prepare_rest(q_codes, q_exps.T, *lin, seq_count)
    arrived = exchange(packed)
    own = after(own, packed)
    onward = [(i + 2 - i % 2 * 4) % count for i in range(count)]
    first = lax.ppermute(own, "head", list(enumerate(onward)))
    second = lax.ppermute(own, "head", [(to, i) for i, to in enumerate(onward)])
    partner = core_swap(own)
    far = lax.ppermute(first, "head", list(enumerate(onward)))
    far_other = lax.ppermute(first, "head", [(i, to ^ 1) for i, to in enumerate(onward)])
    arrived = after(arrived, first, second)
    first_other = core_swap(after(first, second))
    second_other = core_swap(second)
    state = attend(
        ranks((0, 0), (0, 1), (-1, 0), (1, 1), (1, 0), (-1, 1)),
        arrived,
        [own, partner, first, first_other, second, second_other],
        None,
        span,
    )
    entering = entering_states(after(arrived, state[0]), tokens)
    attended = attend(
        ranks((2, 0), (2, 1)), arrived, [far, far_other], state, span, tail=entering
    )
    returned = exchange(attended)
    return tuple(finish(returned, tokens, inner, decayed, before, fades))


def solution(mesh):
    rows = P(("seq", "head"), None)
    tiles = P("seq", "head")
    return jax.shard_map(
        shards,
        mesh=mesh,
        in_specs=(rows,) * 6 + (tiles,) * 4,
        out_specs=(rows, tiles),
        check_vma=False,
    )
```
